256 devices in a mesh: grp: 16 (over z_hi, y, core), dev: 16 (over z_lo, x).
Axes of the slice: x: 4, y: 4, z: 8 (z_hi: 2, z_lo: 4; z = z_hi * 4 + z_lo), core: 2. Of those that a mesh axis runs over, the one named last changes fastest.
Arguments:
- tokens: bfloat16 [2048, 4096], P('grp', 'dev'), may hold values from -6 to 6
- norm_gain: float32 [4096], replicated, may hold values from 0.1 to 1.9
- gate_weight: bfloat16 [4096, 6144], P('grp', 'dev'), may hold values from -0.09375 to 0.09375
- up_weight: bfloat16 [4096, 6144], P('grp', 'dev'), may hold values from -0.09375 to 0.09375
- down_weight: bfloat16 [6144, 4096], P('dev', 'grp'), may hold values from -0.078125 to 0.078125
- out_cotangent: bfloat16 [2048, 4096], P('grp', 'dev'), may hold values from -6 to 6
Outputs:
- mixed_out: bfloat16 [2048, 4096], P('grp', 'dev')
- d_tokens: float32 [2048, 4096], P('grp', 'dev')
- grad_gate: float32 [4096, 6144], P('grp', 'dev')
- grad_up: float32 [4096, 6144], P('grp', 'dev')
- grad_down: float32 [6144, 4096], P('dev', 'grp')
The draws below stay inside these ranges and needn't reach their ends.
All inputs are finite; a program needn't handle non-finite values.
Results may differ from the reference program's by a relative error of at most 0.022.
Values may be sent and summed in bfloat16 or wider, within the bound.
No kernel may reach another device: no remote copies, remote signals or barrier semaphores. Data moves between devices by JAX's collectives and lax.ppermute only.
A program may use at most 64 MiB of HBM per device.

```python
import jax
import jax.numpy as jnp
from jax import lax

D = 4096
FFW = 6144
TOKENS = 2048
N_DEV = 16


def raised(array, rng, source, target, shards_of, factor):
    owner, partner = [(jnp.arange(array.shape[axis_at]) // (array.shape[axis_at] // shards_of)).reshape([-1 if axis == axis_at else 1 for axis in range(array.ndim)]) for axis_at in (source, target)]
    chosen = jax.random.permutation(rng, shards_of)[partner]
    strong = (owner == chosen) | (owner == (partner + shards_of // 2) % shards_of)
    return jnp.where(strong, factor * array, array)


def block_scale(stream_key, shape, cuts, low, top_value):
    loudness, own = 1.0, jax.random.fold_in(stream_key, 6)
    for axis_at, blocks in cuts:
        draws = jnp.exp(jax.random.uniform(jax.random.fold_in(own, axis_at), (blocks,), jnp.float32, low / len(cuts), top_value / len(cuts)))
        loudness = loudness * jnp.repeat(draws, shape[axis_at] // blocks).reshape([-1 if axis == axis_at else 1 for axis in range(len(shape))])
    return loudness


def centred(stream_key, extent, scale, bound, cuts=(), held_as=jnp.bfloat16):
    result = jax.random.normal(stream_key, extent, jnp.float32) * scale
    if len(cuts) > 0:
        result = block_scale(stream_key, extent, cuts, -0.22, 0.18) * result
    return jnp.clip(result, min=-bound, max=bound).astype(held_as)


def gaussian_with(stream_key, shape, spread, limit, shards, heavy, held_as=jnp.bfloat16):
    array = spread * jax.random.normal(stream_key, shape, jnp.float32)
    if shards:
        array = array * block_scale(stream_key, shape, shards, -0.22, 0.18)
    return jnp.clip(raised(array, jax.random.fold_in(stream_key, 3), *heavy), -limit, limit).astype(held_as)


def setup_inputs(seed: int = 0) -> dict:
    arg_keys = jax.random.split(jax.random.key(seed), 7)
    return {
        "tokens": gaussian_with(arg_keys[0], (TOKENS, D), 1.0, 6.0, ((0, 16), (1, 16)), (0, 1, 16, 2.0)),
        "norm_gain": jnp.clip(1.0 + 0.18 * jax.random.normal(arg_keys[1], (D,), jnp.float32), 0.1, 1.9),
        "gate_weight": centred(arg_keys[2], (D, FFW), D ** -0.5, 0.09375, ((0, 16), (1, 16))),
        "up_weight": centred(arg_keys[3], (D, FFW), D ** -0.5, 0.09375, ((0, 16), (1, 16))),
        "down_weight": centred(arg_keys[4], (FFW, D), FFW ** -0.5, 0.078125, ((0, 16), (1, 16))),
        "out_cotangent": gaussian_with(arg_keys[5], (TOKENS, D), 1.0, 6.0, ((0, 16), (1, 16)), (0, 1, 16, 2.0)),
    }


norm_epsilon = 1e-06

def gelu_tanh(value):
    return jax.nn.gelu(value, approximate=True)

def rounded(term):
    return lax.optimization_barrier(term.astype(jnp.bfloat16)).astype(jnp.float32)

def reference(tokens, norm_gain, gate_weight, up_weight, down_weight, out_cotangent):
    full_float = tokens.astype(jnp.float32)
    inv_rms = lax.rsqrt(lax.optimization_barrier(jnp.mean(full_float * full_float, axis=1, keepdims=True)) + norm_epsilon)
    normed = full_float * inv_rms
    hidden_in = (normed * norm_gain).astype(jnp.bfloat16)
    gate_pre = jnp.dot(hidden_in, gate_weight, preferred_element_type=jnp.float32)
    up_pre = jnp.dot(hidden_in, up_weight, preferred_element_type=jnp.float32)
    activated, pullback = jax.vjp(gelu_tanh, gate_pre)
    inner_act = (activated * up_pre).astype(jnp.bfloat16)
    block_width = FFW // N_DEV
    branch = jnp.zeros(full_float.shape, jnp.float32)
    for block in range(N_DEV):
        lower = block * block_width
        upper = lower + block_width
        branch = branch + rounded(jnp.dot(inner_act[:, lower:upper], down_weight[lower:upper, :], preferred_element_type=jnp.float32))
    mixed_out = (full_float + branch).astype(jnp.bfloat16)
    d_inner = lax.dot_general(out_cotangent, down_weight, (((1,), (1,)), ((), ())), preferred_element_type=jnp.float32)
    d_gate = pullback(d_inner * up_pre)[0].astype(jnp.bfloat16)
    d_up = (d_inner * activated).astype(jnp.bfloat16)
    grad_down = lax.dot_general(inner_act, out_cotangent, (((0,), (0,)), ((), ())), preferred_element_type=jnp.float32)
    grad_gate = lax.dot_general(hidden_in, d_gate, (((0,), (0,)), ((), ())), preferred_element_type=jnp.float32)
    grad_up = lax.dot_general(hidden_in, d_up, (((0,), (0,)), ((), ())), preferred_element_type=jnp.float32)
    feat_grad = jnp.zeros(full_float.shape, jnp.float32)
    for block in range(N_DEV):
        lower = block * block_width
        upper = lower + block_width
        first = lax.dot_general(d_gate[:, lower:upper], gate_weight[:, lower:upper], (((1,), (1,)), ((), ())), preferred_element_type=jnp.float32)
        second = lax.dot_general(d_up[:, lower:upper], up_weight[:, lower:upper], (((1,), (1,)), ((), ())), preferred_element_type=jnp.float32)
        feat_grad = feat_grad + rounded(first + second)
    d_norm = feat_grad * norm_gain
    mean_term = lax.optimization_barrier(jnp.mean(d_norm * normed, axis=1, keepdims=True))
    d_tokens = out_cotangent.astype(jnp.float32) + inv_rms * (d_norm - normed * mean_term)
    return (mixed_out, d_tokens, grad_gate, grad_up, grad_down)
```

```python
import jax
import jax.numpy as jnp
from jax import lax
from jax.sharding import Mesh
from jax.sharding import PartitionSpec as P

norm_epsilon = 1e-06
F32 = jnp.float32
BF16 = jnp.bfloat16


def gelu_tanh(value):
    return jax.nn.gelu(value, approximate=True)


def dot(left, right, left_dim, right_dim):
    return lax.dot_general(
        left, right, (((left_dim,), (right_dim,)), ((), ())), preferred_element_type=F32
    )


def shift(array, axis, by):
    return lax.ppermute(array, axis, [(i, (i + by) % 4) for i in range(4)])


def swap(array, axis):
    return lax.ppermute(array, axis, [(0, 1), (1, 0)])


def z_pairs(k1, k2):
    return [
        (4 * zs + 2 * h + l, 4 * h + 2 * (zs ^ k1) + (l ^ k2))
        for zs in range(2)
        for h in range(2)
        for l in range(2)
    ]


def z_gather(block):
    return jnp.stack(
        [
            lax.ppermute(block, ("zh", "zl"), z_pairs(k1, k2))
            for k1 in range(2)
            for k2 in range(2)
        ]
    )


def z_scatter(blocks):
    parts = [
        lax.ppermute(blocks[2 * k1 + k2], ("zh", "zl"), [(t, s) for s, t in z_pairs(k1, k2)])
        for k1 in range(2)
        for k2 in range(2)
    ]
    return sum(p.astype(F32) for p in parts)


def x_gather(blocks):
    return jnp.stack([blocks] + [shift(blocks, "x", s) for s in (1, 2, 3)])


def scatter(parts, axis):
    total = parts[0].astype(F32)
    for s in (1, 2, 3):
        total = total + shift(parts[s], axis, -s).astype(F32)
    return total


def pick(array, index):
    return lax.dynamic_index_in_dim(array, index, 0, keepdims=False)


def on_device(tokens, norm_gain, gate_weight, up_weight, down_weight, out_cotangent):
    zh, y, c, zl, x = (lax.axis_index(n) for n in ("zh", "y", "c", "zl", "x"))
    a, b = zl // 2, zl % 2
    own = a ^ zh

    weights = jnp.concatenate([gate_weight, up_weight, down_weight.T], axis=1)
    by_y = jnp.stack([weights] + [shift(weights, "y", t) for t in (1, 2, 3)])
    by_cy = jnp.concatenate([by_y, swap(by_y, "c")])

    order = []
    for s in range(4):
        for k2 in range(2):
            order.append((b ^ k2) * 4 + (x - s) % 4)
    w_rel = jnp.concatenate([pick(by_cy, (c ^ (q % 2)) * 4 + (y - q // 2) % 4) for q in order])
    gain8 = norm_gain.reshape(2, 8, 256)[zh]
    gain_rel = jnp.concatenate([pick(gain8, q) for q in order])

    def gather(block):
        pieces = x_gather(z_gather(block)).reshape(4, 2, 2, 128, 256)
        return pieces.transpose(1, 3, 0, 2, 4).reshape(256, 2048)

    tok = gather(tokens).astype(F32)
    squares = jnp.sum(tok * tok, axis=1).reshape(2, 128)
    xg = (tok * gain_rel).astype(BF16)
    part = dot(xg, w_rel[:, :768], 1, 0).astype(BF16).reshape(2, 128, 768)
    total = pick(squares, own) + swap(pick(squares, 1 - own), "zh")
    inv_rms = lax.rsqrt(total / 4096 + norm_epsilon)[:, None]
    pre = pick(part, own).astype(F32) + swap(pick(part, 1 - own), "zh").astype(F32)
    pre = pre * inv_rms
    gate_pre, up_pre = pre[:, :384], pre[:, 384:]
    activated, pullback = jax.vjp(gelu_tanh, gate_pre)
    inner_own = (activated * up_pre).astype(BF16)

    def both(mine):
        other = swap(mine, "zh")
        return jnp.where(own == 0, jnp.concatenate([mine, other]), jnp.concatenate([other, mine]))

    inner = both(inner_own)

    def reduce_out(partial):
        pieces = partial.astype(BF16).reshape(2, 128, 4, 2, 256).transpose(2, 0, 3, 1, 4)
        return z_scatter(scatter(pieces, "x").astype(BF16).reshape(4, 128, 256))

    branch = reduce_out(dot(inner, w_rel[:, 768:], 1, 1))
    local = tokens.astype(F32)
    mixed_out = (local + branch).astype(BF16)

    cot = gather(out_cotangent)
    part = dot(cot, w_rel[:, 768:], 1, 0).astype(BF16).reshape(2, 128, 384)
    d_inner = pick(part, own).astype(F32) + swap(pick(part, 1 - own), "zh").astype(F32)
    d_scaled = d_inner * inv_rms
    d_gate = pullback(d_scaled * up_pre)[0].astype(BF16)
    d_up = (d_scaled * activated).astype(BF16)
    tau = jnp.sum(d_gate.astype(F32) * gate_pre + d_up.astype(F32) * up_pre, axis=1)
    tau = scatter([tau] * 4, "x")
    tau = scatter([tau] * 4, "zl")
    d_both = both(jnp.concatenate([d_gate, d_up], axis=1))
    feat = reduce_out(dot(d_both, w_rel[:, :768], 1, 1))
    gain_own = lax.dynamic_slice_in_dim(norm_gain, (zl * 4 + x) * 256, 256, 0)
    coef = inv_rms * (tau / 4096)[:, None]
    d_tokens = out_cotangent.astype(F32) + feat * gain_own - local * coef

    def reduce_grad(partial):
        blocks = partial.astype(BF16).reshape(8, 256, -1)

        def block_of(t, cc):
            q = ((y - t) % 4) * 2 + (c ^ cc)
            return pick(blocks, ((x - q % 4) % 4) * 2 + (b ^ (q // 4)))

        mine = jnp.stack([block_of(t, 0) for t in range(4)])
        theirs = jnp.stack([block_of(t, 1) for t in range(4)])
        summed = (mine.astype(F32) + swap(theirs, "c").astype(F32)).astype(BF16)
        return scatter(summed, "y")

    grad_down = reduce_grad(dot(cot, inner, 0, 0)).T
    grads = reduce_grad(dot(xg, d_both, 0, 0))
    return (mixed_out, d_tokens, grads[:, :384], grads[:, 384:], grad_down)


def solution(mesh):
    split = Mesh(mesh.devices.reshape(2, 4, 2, 4, 4), ("zh", "y", "c", "zl", "x"))
    grp, dev = ("zh", "y", "c"), ("zl", "x")
    in_specs = (P(grp, dev), P(), P(grp, dev), P(grp, dev), P(dev, grp), P(grp, dev))
    out_specs = (P(grp, dev), P(grp, dev), P(grp, dev), P(grp, dev), P(dev, grp))
    return jax.shard_map(
        on_device, mesh=split, in_specs=in_specs, out_specs=out_specs, check_vma=False
    )
```

```python
import functools

import jax
import jax.numpy as jnp
from jax import lax
from jax.experimental import pallas as pl
from jax.experimental.pallas import tpu as pltpu
from jax.sharding import Mesh
from jax.sharding import PartitionSpec as P

norm_epsilon = 1e-06
F32 = jnp.float32
BF16 = jnp.bfloat16
ANY = pl.BlockSpec(memory_space=pl.ANY)
SMEM = pl.BlockSpec(memory_space=pltpu.SMEM)
VMEM = pl.BlockSpec(memory_space=pltpu.VMEM)
MIB = 1 << 20


def dot(left, right, left_dim, right_dim):
    return lax.dot_general(
        left, right, (((left_dim,), (right_dim,)), ((), ())), preferred_element_type=F32
    )


def shift(array, axis, by):
    return lax.ppermute(array, axis, [(i, (i + by) % 4) for i in range(4)])


def swap(array, axis):
    return lax.ppermute(array, axis, [(0, 1), (1, 0)])


def z_pairs(k):
    k1, k2 = k // 2, k % 2
    return [
        (4 * zs + 2 * h + l, 4 * h + 2 * (zs ^ k1) + (l ^ k2))
        for zs in range(2)
        for h in range(2)
        for l in range(2)
    ]


def split_float(value):
    head = value.astype(BF16).astype(F32)
    return head, value - head


def call(body, ids, operands, specs, outs, scratch=(), limit=8):
    return pl.pallas_call(
        body,
        out_shape=[jax.ShapeDtypeStruct(s, d) for s, d in outs],
        in_specs=[SMEM] + specs,
        out_specs=[VMEM] * len(outs),
        scratch_shapes=list(scratch),
        compiler_params=pltpu.CompilerParams(vmem_limit_bytes=limit * MIB),
    )(ids, *operands)


def block_q(ids, t, cc):
    return lax.rem(ids[1] - t + 4, 4) * 2 + (ids[2] ^ cc)


def products_kernel(ids, *refs):
    pieces, weights, gain = refs[:4], refs[4:12], refs[12]
    send, keep, squares, mixed = refs[13:17]
    x_all, w_all, acc, sq, x_sem, w_sem = refs[17:]
    x_copies = [pltpu.make_async_copy(pieces[s], x_all.at[s], x_sem.at[s]) for s in range(4)]
    w_copies = [pltpu.make_async_copy(weights[i], w_all.at[:, i], w_sem.at[i]) for i in range(8)]
    for copy in x_copies + w_copies:
        copy.start()
    for copy in x_copies:
        copy.wait()
    low = ids[3] % 2
    own = (ids[3] // 2) ^ ids[0]
    total = [jnp.zeros((128, 1), F32) for _ in range(2)]
    for i in range(8):
        q = block_q(ids, i % 4, i // 4)
        s = lax.rem(ids[4] - lax.rem(q, 4) + 4, 4)
        k2 = low ^ (q // 4)
        row = gain[ids[0] * 8 + q]
        for k1 in range(2):
            value = x_all[s, 2 * k1 + k2, 0].astype(F32)
            total[k1] = total[k1] + jnp.sum(value * value, axis=1, keepdims=True)
            at = (slice(128 * k1, 128 * k1 + 128), slice(256 * i, 256 * i + 256))
            mixed[(0,) + at] = (value * row).astype(BF16)
            mixed[(1,) + at] = x_all[s, 2 * k1 + k2, 1]
    for copy in w_copies:
        copy.wait()
    for k1 in range(2):
        sq[k1] = jnp.broadcast_to(total[k1], (128, 128))
    for w in range(3):
        left = mixed[0 if w < 2 else 1]
        part = dot(left, w_all[w].reshape(2048, 384), 1, 0)
        acc[:, :, 384 * w : 384 * w + 384] = part.reshape(2, 128, 384)
    keep[...] = acc[own]
    squares[...] = sq[own]
    send[:, :1152] = acc[1 - own].astype(BF16)
    head, rest = split_float(sq[1 - own])
    lane = lax.broadcasted_iota(jnp.int32, (128, 128), 1)
    send[:, 1152:] = jnp.where(lane < 64, head, rest).astype(BF16)


def activation_kernel(ids, keep, squares, recv, mine, scale):
    total = squares[:, 0:1] + recv[:, 1152:1153].astype(F32) + recv[:, 1216:1217].astype(F32)
    inv_rms = lax.rsqrt(total / 4096 + norm_epsilon)
    scale[...] = jnp.broadcast_to(inv_rms, (128, 128))
    gate = (keep[:, :384] + recv[:, :384].astype(F32)) * inv_rms
    up = (keep[:, 384:768] + recv[:, 384:768].astype(F32)) * inv_rms
    d_inner = (keep[:, 768:] + recv[:, 768:1152].astype(F32)) * inv_rms
    root = 0.7978845608028654
    tanh = jnp.tanh(root * (gate + 0.044715 * (gate * gate * gate)))
    cdf = 0.5 * (1.0 + tanh)
    activated = gate * cdf
    slope = cdf + 0.5 * gate * (1.0 - tanh * tanh) * root * (1.0 + 3 * 0.044715 * (gate * gate))
    d_gate = (d_inner * up * slope).astype(BF16)
    d_up = (d_inner * activated).astype(BF16)
    mine[:128, :384] = (activated * up).astype(BF16)
    mine[:128, 384:768] = d_gate
    mine[:128, 768:] = d_up
    tau = jnp.sum(d_gate.astype(F32) * gate + d_up.astype(F32) * up, axis=1, keepdims=True)
    rows = jnp.broadcast_to(tau, (128, 128)).T[:16]
    head, rest = split_float(rows)
    mine[128:, :] = jnp.zeros((16, 1152), BF16)
    mine[128:, :128] = head.astype(BF16)
    mine[128:, 128:256] = rest.astype(BF16)


def load_rows(ids, mine, recv, d_all):
    own = (ids[3] // 2) ^ ids[0]
    d_all[own] = mine[...]
    d_all[1 - own] = recv[...]


def outputs_kernel(ids, mine, recv, *refs):
    weights, outs, (w_all, d_all, w_sem) = refs[:8], refs[8:12], refs[12:]
    copies = [pltpu.make_async_copy(weights[i], w_all.at[:, i], w_sem.at[i]) for i in range(8)]
    for copy in copies:
        copy.start()
    load_rows(ids, mine, recv, d_all)
    for copy in copies:
        copy.wait()
    low = ids[3] % 2
    acts = [d_all[:, :128, 384 * w : 384 * w + 384].reshape(256, 384) for w in range(3)]
    for s in range(4):
        for k2 in range(2):
            q = (low ^ k2) * 4 + lax.rem(ids[4] - s + 4, 4)
            t = lax.rem(ids[1] - q // 2 + 4, 4)
            i = (ids[2] ^ lax.rem(q, 2)) * 4 + t
            branch = dot(acts[0], w_all[2, i], 1, 1).astype(BF16)
            feat = dot(acts[1], w_all[0, i], 1, 1) + dot(acts[2], w_all[1, i], 1, 1)
            feat = feat.astype(BF16)
            for k1 in range(2):
                rows = slice(128 * k1, 128 * k1 + 128)
                outs[s][2 * k1 + k2, :128] = branch[rows]
                outs[s][2 * k1 + k2, 128:256] = feat[rows]
                outs[s][2 * k1 + k2, 256:] = d_all[k1, 128:, :256]


def gradients_kernel(ids, mine, recv, mixed, kept, sent, d_all):
    load_rows(ids, mine, recv, d_all)
    for w, a in ((0, 1), (1, 2), (2, 0)):
        right = d_all[:, :128, 384 * a : 384 * a + 384].reshape(256, 384)
        for cc, out in ((0, kept), (1, sent)):
            left = mixed[0 if w < 2 else 1, :, 1024 * cc : 1024 * cc + 1024]
            out[w] = dot(left, right, 0, 0).astype(BF16).reshape(4, 256, 384)


def core_sum_kernel(ids, kept, recv, *outs):
    for t in range(4):
        outs[t][...] = (kept[:, t].astype(F32) + recv[:, t].astype(F32)).astype(BF16)


def sum_refs(refs, at):
    total = refs[0][at].astype(F32)
    for ref in refs[1:]:
        total = total + ref[at].astype(F32)
    return total


def x_sum_kernel(ids, *refs):
    parts, outs = refs[:4], refs[4:]
    for k in range(4):
        outs[k][:256] = sum_refs(parts, (k, slice(0, 256))).astype(BF16)
        tail = sum_refs(parts, (k, slice(256, 272)))
        head, rest = split_float(tail[:, :128] + tail[:, 128:])
        outs[k][256:, :128] = head.astype(BF16)
        outs[k][256:, 128:] = rest.astype(BF16)


def finish_kernel(ids, p0, p1, p2, p3, tokens, cot, gain, scale, mixed_out, d_tokens):
    parts = (p0, p1, p2, p3)
    local = tokens[...].astype(F32)
    mixed_out[...] = (local + sum_refs(parts, slice(0, 128))).astype(BF16)
    tail = sum_refs(parts, slice(256, 272))
    tau = (tail[:, :128] + tail[:, 128:])[0:1]
    tau = jnp.broadcast_to(tau, (128, 128)).T
    coef = (scale[...] * tau * (1.0 / 4096))[:, 0:1]
    feat = sum_refs(parts, slice(128, 256)) * gain[ids[3] * 4 + ids[4]]
    d_tokens[...] = cot[...].astype(F32) + feat - local * coef


def grads_sum_kernel(ids, p0, p1, p2, p3, grad_gate, grad_up, grad_down):
    parts = (p0, p1, p2, p3)
    grad_gate[...] = sum_refs(parts, 0)
    grad_up[...] = sum_refs(parts, 1)
    grad_down[...] = sum_refs(parts, 2).T


def on_device(tokens, norm_gain, gate_weight, up_weight, down_weight, out_cotangent):
    ids = jnp.stack([lax.axis_index(n) for n in ("zh", "y", "c", "zl", "x")]).astype(jnp.int32)
    gain = norm_gain.reshape(16, 1, 256)

    pair = jnp.stack([tokens, out_cotangent])
    by_z = jnp.stack([lax.ppermute(pair, ("zh", "zl"), z_pairs(k)) for k in range(4)])
    pieces = [by_z] + [shift(by_z, "x", s) for s in (1, 2, 3)]
    weights = jnp.stack([gate_weight, up_weight, down_weight.T])
    by_y = [weights] + [shift(weights, "y", t) for t in (1, 2, 3)]
    w_blocks = by_y + [swap(piece, "c") for piece in by_y]

    send, keep, squares, mixed = call(
        products_kernel,
        ids,
        [*pieces, *w_blocks, gain],
        [ANY] * 12 + [VMEM],
        [((128, 1280), BF16), ((128, 1152), F32), ((128, 128), F32), ((2, 256, 2048), BF16)],
        [
            pltpu.VMEM((4, 4, 2, 128, 256), BF16),
            pltpu.VMEM((3, 8, 256, 384), BF16),
            pltpu.VMEM((2, 128, 1152), F32),
            pltpu.VMEM((2, 128, 128), F32),
            pltpu.SemaphoreType.DMA((4,)),
            pltpu.SemaphoreType.DMA((8,)),
        ],
        32,
    )
    mine, scale = call(
        activation_kernel,
        ids,
        [keep, squares, swap(send, "zh")],
        [VMEM] * 3,
        [((144, 1152), BF16), ((128, 128), F32)],
    )
    theirs = swap(mine, "zh")
    rows = pltpu.VMEM((2, 144, 1152), BF16)
    parts = call(
        outputs_kernel,
        ids,
        [mine, theirs, *w_blocks],
        [VMEM] * 2 + [ANY] * 8,
        [((4, 272, 256), BF16)] * 4,
        [pltpu.VMEM((3, 8, 256, 384), BF16), rows, pltpu.SemaphoreType.DMA((8,))],
        24,
    )
    kept, sent = call(
        gradients_kernel,
        ids,
        [mine, theirs, mixed],
        [VMEM] * 3,
        [((3, 4, 256, 384), BF16)] * 2,
        [rows],
        32,
    )
    parts = [parts[0]] + [shift(parts[s], "x", -s) for s in (1, 2, 3)]
    blocks = call(x_sum_kernel, ids, parts, [VMEM] * 4, [((272, 256), BF16)] * 4)
    blocks = [
        lax.ppermute(blocks[k], ("zh", "zl"), [(t, s) for s, t in z_pairs(k)]) for k in range(4)
    ]
    mixed_out, d_tokens = call(
        finish_kernel,
        ids,
        [*blocks, tokens, out_cotangent, gain, scale],
        [VMEM] * 8,
        [((128, 256), BF16), ((128, 256), F32)],
    )
    sums = call(
        core_sum_kernel, ids, [kept, swap(sent, "c")], [VMEM] * 2, [((3, 256, 384), BF16)] * 4, (), 16
    )
    sums = [sums[0]] + [shift(sums[t], "y", -t) for t in (1, 2, 3)]
    grad_gate, grad_up, grad_down = call(
        grads_sum_kernel,
        ids,
        sums,
        [VMEM] * 4,
        [((256, 384), F32), ((256, 384), F32), ((384, 256), F32)],
        (),
        16,
    )
    return (mixed_out, d_tokens, grad_gate, grad_up, grad_down)


def solution(mesh):
    split = Mesh(mesh.devices.reshape(2, 4, 2, 4, 4), ("zh", "y", "c", "zl", "x"))
    grp, dev = ("zh", "y", "c"), ("zl", "x")
    in_specs = (P(grp, dev), P(), P(grp, dev), P(grp, dev), P(dev, grp), P(grp, dev))
    out_specs = (P(grp, dev), P(grp, dev), P(grp, dev), P(grp, dev), P(dev, grp))
    return jax.shard_map(
        on_device, mesh=split, in_specs=in_specs, out_specs=out_specs, check_vma=False
    )
```

```python
import math

import jax
import jax.numpy as jnp
from jax import lax
from jax.experimental import pallas as pl
from jax.experimental.pallas import tpu as pltpu
from jax.sharding import Mesh
from jax.sharding import PartitionSpec as P

norm_epsilon = 1e-06
F32 = jnp.float32
BF16 = jnp.bfloat16
ANY = pl.BlockSpec(memory_space=pl.ANY)
HBM = pl.BlockSpec(memory_space=pltpu.HBM)
SMEM = pl.BlockSpec(memory_space=pltpu.SMEM)
VMEM = pl.BlockSpec(memory_space=pltpu.VMEM)
MIB = 1 << 20


def dot(left, right, left_dim, right_dim):
    return lax.dot_general(
        left, right, (((left_dim,), (right_dim,)), ((), ())), preferred_element_type=F32
    )


def shift(array, axis, by):
    return lax.ppermute(array, axis, [(i, (i + by) % 4) for i in range(4)])


def swap(array, axis):
    return lax.ppermute(array, axis, [(0, 1), (1, 0)])


def z_pairs(k):
    k1, k2 = k // 2, k % 2
    return [
        (4 * zs + 2 * h + l, 4 * h + 2 * (zs ^ k1) + (l ^ k2))
        for zs in range(2)
        for h in range(2)
        for l in range(2)
    ]


def split_float(value):
    head = value.astype(BF16).astype(F32)
    return head, value - head


def call(body, ids, operands, specs, outs, scratch=(), limit=8, flops=0):
    size = sum(a.size * a.dtype.itemsize for a in operands)
    size += sum(2 * math.prod(shape) for shape, _ in outs)
    return pl.pallas_call(
        body,
        out_shape=[jax.ShapeDtypeStruct(s, d) for s, d in outs],
        in_specs=[SMEM] + specs,
        out_specs=[VMEM] * len(outs),
        scratch_shapes=list(scratch),
        compiler_params=pltpu.CompilerParams(vmem_limit_bytes=limit * MIB),
        cost_estimate=pl.CostEstimate(flops=flops, bytes_accessed=size, transcendentals=0),
    )(ids, *operands)


def block_q(ids, i):
    return lax.rem(ids[1] - i % 4 + 4, 4) * 2 + (ids[2] ^ (i // 4))


def block_i(ids, s, k2):
    q = ((ids[3] % 2) ^ k2) * 4 + lax.rem(ids[4] - s + 4, 4)
    return (ids[2] ^ lax.rem(q, 2)) * 4 + lax.rem(ids[1] - q // 2 + 4, 4)


def weight_copies(weights, rows, w_all, sem):
    first, count = rows
    return [
        pltpu.make_async_copy(view.at[pl.ds(first, count)], w_all.at[:, i], sem.at[i])
        for i, view in enumerate(weights)
    ]


def pack_kernel(ids, tokens, cot, gate, up, down, pair, own, down_in, sem):
    moves = [(down, down_in), (tokens, pair.at[0]), (cot, pair.at[1])]
    moves += [(gate, own.at[0]), (up, own.at[1])]
    copies = [pltpu.make_async_copy(*move, sem.at[i]) for i, move in enumerate(moves)]
    for copy in copies:
        copy.start()
    copies[0].wait()
    own[2] = down_in[...].T
    for copy in copies[1:]:
        copy.wait()


def stack_kernel(ids, p0, p1, p2, p3, tokens, cot):
    for k, piece in enumerate((p0, p1, p2, p3)):
        tokens[k] = piece[0]
        cot[k] = piece[1]


def load_pieces(ids, pieces, x_all, x_sem):
    copies = [pltpu.make_async_copy(pieces[s], x_all.at[s], x_sem.at[s]) for s in range(4)]
    for copy in copies:
        copy.start()
    for copy in copies:
        copy.wait()


def blocks_of(ids, x_all):
    for i in range(8):
        q = block_q(ids, i)
        s = lax.rem(ids[4] - lax.rem(q, 4) + 4, 4)
        k2 = (ids[3] % 2) ^ (q // 4)
        for k1 in range(2):
            at = (slice(128 * k1, 128 * k1 + 128), slice(256 * i, 256 * i + 256))
            yield i, q, k1, at, x_all[s, 2 * k1 + k2]


def forward_products_kernel(ids, *refs):
    pieces, weights, gain, send, mixed = refs[:4], refs[4:12], refs[12], refs[13], refs[14]
    x_all, w_all, x_sem, w_sem = refs[15:]
    copies = weight_copies(weights, (0, 2), w_all, w_sem)
    for copy in copies:
        copy.start()
    load_pieces(ids, pieces, x_all, x_sem)
    total = [jnp.zeros((128, 1), F32) for _ in range(2)]
    for i, q, k1, at, block in blocks_of(ids, x_all):
        value = block.astype(F32)
        total[k1] = total[k1] + jnp.sum(value * value, axis=1, keepdims=True)
        mixed[at] = (value * gain[ids[0] * 8 + q]).astype(BF16)
    for copy in copies:
        copy.wait()
    for w in range(2):
        part = dot(mixed[...], w_all[w].reshape(2048, 384), 1, 0)
        send[:256, 384 * w : 384 * w + 384] = part.astype(BF16)
    send[256:, :] = jnp.zeros((16, 768), BF16)
    for k1 in range(2):
        head, rest = split_float(jnp.broadcast_to(total[k1], (128, 128)).T[:16])
        send[256:, 128 * k1 : 128 * k1 + 128] = head.astype(BF16)
        send[256:, 256 + 128 * k1 : 384 + 128 * k1] = rest.astype(BF16)


def backward_products_kernel(ids, *refs):
    pieces, weights, send, mixed = refs[:4], refs[4:12], refs[12], refs[13]
    x_all, w_all, x_sem, w_sem = refs[14:]
    copies = weight_copies(weights, (2, 1), w_all, w_sem)
    for copy in copies:
        copy.start()
    load_pieces(ids, pieces, x_all, x_sem)
    for i, q, k1, at, block in blocks_of(ids, x_all):
        mixed[at] = block
    for copy in copies:
        copy.wait()
    part = dot(mixed[...], w_all[0].reshape(2048, 384), 1, 0)
    send[...] = part.astype(BF16)


def activations(mine, recv):
    tail = mine[256:257].astype(F32) + recv[256:257].astype(F32)
    total = jnp.concatenate([tail[:, :128] + tail[:, 256:384], tail[:, 128:256] + tail[:, 384:512]])
    cols = [jnp.broadcast_to(total[k : k + 1], (128, 128)).T[:, 0:1] for k in range(2)]
    inv_rms = lax.rsqrt(jnp.concatenate(cols) / 4096 + norm_epsilon)
    pre = (mine[:256].astype(F32) + recv[:256].astype(F32)) * inv_rms
    gate, up = pre[:, :384], pre[:, 384:]
    root = 0.7978845608028654
    tanh = jnp.tanh(root * (gate + 0.044715 * (gate * gate * gate)))
    cdf = 0.5 * (1.0 + tanh)
    slope = cdf + 0.5 * gate * (1.0 - tanh * tanh) * root * (1.0 + 3 * 0.044715 * (gate * gate))
    return inv_rms, gate, up, gate * cdf, slope


def gradients_kernel(
    ids, mine, recv, d_mine, d_recv, tokens, cot, kept, sent, acts, scale, tail
):
    inv_rms, gate, up, activated, slope = activations(mine, recv)
    d_inner = (d_mine[...].astype(F32) + d_recv[...].astype(F32)) * inv_rms
    d_gate = (d_inner * up * slope).astype(BF16)
    d_up = (d_inner * activated).astype(BF16)
    acts[:, :384] = d_gate
    acts[:, 384:768] = d_up
    acts[:, 768:] = (activated * up).astype(BF16)
    own = (ids[3] // 2) ^ ids[0]
    picked = jnp.where(own == 0, inv_rms[:128], inv_rms[128:])
    scale[...] = jnp.broadcast_to(picked, (128, 128))
    tau = jnp.sum(d_gate.astype(F32) * gate + d_up.astype(F32) * up, axis=1, keepdims=True)
    for k1 in range(2):
        rows = jnp.broadcast_to(tau[128 * k1 : 128 * k1 + 128], (128, 128)).T[:16]
        head, rest = split_float(rows)
        tail[k1, :, :128] = head.astype(BF16)
        tail[k1, :, 128:] = rest.astype(BF16)
    for cc, out in ((1, sent), (0, kept)):
        for w in range(3):
            right = acts[:, 384 * w : 384 * w + 384]
            source = cot if w == 2 else tokens
            left = source[:, 1024 * cc : 1024 * cc + 1024]
            out[w] = dot(left, right, 0, 0).astype(BF16).reshape(4, 256, 384)


def outputs_kernel(ids, acts, tail, *refs):
    weights, outs, (w_all, w_sem) = refs[:8], refs[8:12], refs[12:]
    copies = weight_copies(weights, (0, 3), w_all, w_sem)
    for copy in copies:
        copy.start()
    for copy in copies:
        copy.wait()
    left = [acts[:, 384 * w : 384 * w + 384] for w in range(3)]
    for s in range(4):
        for k2 in range(2):
            i = block_i(ids, s, k2)
            branch = dot(left[2], w_all[2, i], 1, 1).astype(BF16)
            feat = dot(left[0], w_all[0, i], 1, 1) + dot(left[1], w_all[1, i], 1, 1)
            feat = feat.astype(BF16)
            for k1 in range(2):
                rows = slice(128 * k1, 128 * k1 + 128)
                outs[s][2 * k1 + k2, :128] = branch[rows]
                outs[s][2 * k1 + k2, 128:256] = feat[rows]
                outs[s][2 * k1 + k2, 256:] = tail[k1]


def core_sum_kernel(ids, kept, recv, *outs):
    for t in range(4):
        outs[t][...] = (kept[:, t].astype(F32) + recv[:, t].astype(F32)).astype(BF16)


def sum_refs(refs, at):
    total = refs[0][at].astype(F32)
    for ref in refs[1:]:
        total = total + ref[at].astype(F32)
    return total


def x_sum_kernel(ids, *refs):
    parts, outs = refs[:4], refs[4:]
    for k in range(4):
        outs[k][:256] = sum_refs(parts, (k, slice(0, 256))).astype(BF16)
        tail = sum_refs(parts, (k, slice(256, 272)))
        head, rest = split_float(tail[:, :128] + tail[:, 128:])
        outs[k][256:, :128] = head.astype(BF16)
        outs[k][256:, 128:] = rest.astype(BF16)


def finish_kernel(ids, p0, p1, p2, p3, tokens, cot, gain, scale, mixed_out, d_tokens):
    parts = (p0, p1, p2, p3)
    local = tokens[...].astype(F32)
    mixed_out[...] = (local + sum_refs(parts, slice(0, 128))).astype(BF16)
    tail = sum_refs(parts, slice(256, 272))
    tau = (tail[:, :128] + tail[:, 128:])[0:1]
    tau = jnp.broadcast_to(tau, (128, 128)).T
    coef = (scale[...] * tau * (1.0 / 4096))[:, 0:1]
    feat = sum_refs(parts, slice(128, 256)) * gain[ids[3] * 4 + ids[4]]
    d_tokens[...] = cot[...].astype(F32) + feat - local * coef


def grads_sum_kernel(ids, p0, p1, p2, p3, grad_gate, grad_up, grad_down):
    parts = (p0, p1, p2, p3)
    grad_gate[...] = sum_refs(parts, 0)
    grad_up[...] = sum_refs(parts, 1)
    grad_down[...] = sum_refs(parts, 2).T


def after(value, *events):
    return lax.optimization_barrier((value, *events))[0]


def on_device(tokens, norm_gain, gate_weight, up_weight, down_weight, out_cotangent):
    ids = jnp.stack([lax.axis_index(n) for n in ("zh", "y", "c", "zl", "x")]).astype(jnp.int32)
    gain = norm_gain.reshape(16, 1, 256)
    dma = pltpu.SemaphoreType.DMA

    pair, own = call(
        pack_kernel,
        ids,
        [tokens, out_cotangent, gate_weight, up_weight, down_weight],
        [HBM] * 5,
        [((2, 128, 256), BF16), ((3, 256, 384), BF16)],
        [pltpu.VMEM((384, 256), BF16), dma((5,))],
    )
    by_z = [lax.ppermute(pair, ("zh", "zl"), z_pairs(k)) for k in range(4)]
    tok_z, cot_z = call(stack_kernel, ids, by_z, [VMEM] * 4, [((4, 128, 256), BF16)] * 2)
    y1, y3, _ = lax.optimization_barrier((shift(own, "y", 1), shift(own, "y", 3), tok_z))
    y2 = shift(after(own, y1, y3), "y", 2)
    tok_x = [shift(tok_z, "x", s) for s in (1, 2, 3)]
    y2 = after(y2, *tok_x)
    cot_z = after(cot_z, *tok_x)
    tok_x = [tok_z] + tok_x
    cot_x = [cot_z] + [shift(cot_z, "x", s) for s in (1, 2, 3)]
    by_y = [own, y1, y2, y3]
    weights = by_y + [swap(piece, "c") for piece in by_y]

    x_scratch = [pltpu.VMEM((4, 4, 128, 256), BF16)]
    send, tok_all = call(
        forward_products_kernel,
        ids,
        [*tok_x, *weights, gain],
        [ANY] * 12 + [VMEM],
        [((272, 768), BF16), ((256, 2048), BF16)],
        x_scratch + [pltpu.VMEM((2, 8, 256, 384), BF16), dma((4,)), dma((8,))],
        20,
    )
    d_send, cot_all = call(
        backward_products_kernel,
        ids,
        [*cot_x, *weights],
        [ANY] * 12,
        [((256, 384), BF16), ((256, 2048), BF16)],
        x_scratch + [pltpu.VMEM((1, 8, 256, 384), BF16), dma((4,)), dma((8,))],
        16,
    )
    kept, sent, acts, scale, tail = call(
        gradients_kernel,
        ids,
        [send, swap(send, "zh"), d_send, swap(d_send, "zh"), tok_all, cot_all],
        [VMEM] * 6,
        [((3, 4, 256, 384), BF16)] * 2
        + [((256, 1152), BF16), ((128, 128), F32), ((2, 16, 256), BF16)],
        (),
        24,
        1 << 31,
    )
    parts = call(
        outputs_kernel,
        ids,
        [acts, tail, *weights],
        [VMEM] * 2 + [ANY] * 8,
        [((4, 272, 256), BF16)] * 4,
        [pltpu.VMEM((3, 8, 256, 384), BF16), dma((8,))],
        24,
        1 << 30,
    )
    sums = call(
        core_sum_kernel, ids, [kept, swap(sent, "c")], [VMEM] * 2, [((3, 256, 384), BF16)] * 4, (), 16
    )
    near = [shift(sums[1], "y", -1), shift(sums[3], "y", 1)]
    far = shift(sums[2], "y", 2)
    parts = [parts[0]] + [shift(parts[s], "x", -s) for s in (1, 2, 3)]
    blocks = call(x_sum_kernel, ids, parts, [VMEM] * 4, [((272, 256), BF16)] * 4)
    blocks = [*blocks[:2]] + [after(block, *near) for block in blocks[2:]]
    blocks = [
        lax.ppermute(blocks[k], ("zh", "zl"), [(t, s) for s, t in z_pairs(k)]) for k in range(4)
    ]
    mixed_out, d_tokens = call(
        finish_kernel,
        ids,
        [*blocks, tokens, out_cotangent, gain, scale],
        [VMEM] * 8,
        [((128, 256), BF16), ((128, 256), F32)],
    )
    grad_gate, grad_up, grad_down = call(
        grads_sum_kernel,
        ids,
        [sums[0], near[0], far, near[1]],
        [VMEM] * 4,
        [((256, 384), F32), ((256, 384), F32), ((384, 256), F32)],
        (),
        16,
    )
    return (mixed_out, d_tokens, grad_gate, grad_up, grad_down)


def solution(mesh):
    split = Mesh(mesh.devices.reshape(2, 4, 2, 4, 4), ("zh", "y", "c", "zl", "x"))
    grp, dev = ("zh", "y", "c"), ("zl", "x")
    in_specs = (P(grp, dev), P(), P(grp, dev), P(grp, dev), P(dev, grp), P(grp, dev))
    out_specs = (P(grp, dev), P(grp, dev), P(grp, dev), P(grp, dev), P(dev, grp))
    return jax.shard_map(
        on_device, mesh=split, in_specs=in_specs, out_specs=out_specs, check_vma=False
    )
```

```python
import functools
import math

import jax
import jax.numpy as jnp
from jax import lax
from jax.experimental import pallas as pl
from jax.experimental.pallas import tpu as pltpu
from jax.sharding import Mesh
from jax.sharding import PartitionSpec as P

norm_epsilon = 1e-06
F32 = jnp.float32
BF16 = jnp.bfloat16
SMEM = pl.BlockSpec(memory_space=pltpu.SMEM)
VMEM = pl.BlockSpec(memory_space=pltpu.VMEM)
MIB = 1 << 20


def dot(left, right, left_dim, right_dim):
    return lax.dot_general(
        left, right, (((left_dim,), (right_dim,)), ((), ())), preferred_element_type=F32
    )


def shift(array, axis, by):
    return lax.ppermute(array, axis, [(i, (i + by) % 4) for i in range(4)])


def swap(array, axis):
    return lax.ppermute(array, axis, [(0, 1), (1, 0)])


def z_pairs(k):
    k1, k2 = k // 2, k % 2
    return [
        (4 * zs + 2 * h + l, 4 * h + 2 * (zs ^ k1) + (l ^ k2))
        for zs in range(2)
        for h in range(2)
        for l in range(2)
    ]


def split_float(value):
    head = value.astype(BF16).astype(F32)
    return head, value - head


def call(body, ids, operands, specs, outs, scratch=(), limit=8, flops=0):
    size = sum(a.size * a.dtype.itemsize for a in operands)
    size += sum(2 * math.prod(shape) for shape, _ in outs)
    return pl.pallas_call(
        body,
        out_shape=[jax.ShapeDtypeStruct(s, d) for s, d in outs],
        in_specs=[SMEM] + specs,
        out_specs=[VMEM] * len(outs),
        scratch_shapes=list(scratch),
        compiler_params=pltpu.CompilerParams(vmem_limit_bytes=limit * MIB),
        cost_estimate=pl.CostEstimate(flops=flops, bytes_accessed=size, transcendentals=0),
    )(ids, *operands)


def block_place(ids, i):
    q = lax.rem(ids[1] - i % 4 + 4, 4) * 2 + (ids[2] ^ (i // 4))
    return q, lax.rem(ids[4] - lax.rem(q, 4) + 4, 4), (ids[3] % 2) ^ (q // 4)


def stack_kernel(ids, p0, p1, p2, p3, tokens, cot):
    for k, piece in enumerate((p0, p1, p2, p3)):
        tokens[k] = piece[0]
        cot[k] = piece[1]


def forward_products_kernel(ids, *refs):
    pieces, weights, (gain, send, mixed, x_all, acc) = refs[:4], refs[4:12], refs[12:]
    for s in range(4):
        x_all[s] = pieces[s][...]
    total = [jnp.zeros((128, 1), F32) for _ in range(2)]
    for i in range(8):
        q, s, k2 = block_place(ids, i)
        row = gain[ids[0] * 8 + q]
        at = slice(256 * i, 256 * i + 256)
        for k1 in range(2):
            value = x_all[s, 2 * k1 + k2].astype(F32)
            total[k1] = total[k1] + jnp.sum(value * value, axis=1, keepdims=True)
            mixed[128 * k1 : 128 * k1 + 128, at] = (value * row).astype(BF16)
        for w in range(2):
            part = dot(mixed[:, at], weights[i][w], 1, 0)
            cols = slice(384 * w, 384 * w + 384)
            acc[:, cols] = part if i == 0 else acc[:, cols] + part
    send[:256] = acc[...].astype(BF16)
    send[256:, :] = jnp.zeros((16, 768), BF16)
    for k1 in range(2):
        head, rest = split_float(jnp.broadcast_to(total[k1], (128, 128)).T[:16])
        send[256:, 128 * k1 : 128 * k1 + 128] = head.astype(BF16)
        send[256:, 256 + 128 * k1 : 384 + 128 * k1] = rest.astype(BF16)


def backward_products_kernel(ids, *refs):
    pieces, weights, (send, mixed, x_all, acc) = refs[:4], refs[4:12], refs[12:]
    for s in range(4):
        x_all[s] = pieces[s][...]
    for i in range(8):
        _, s, k2 = block_place(ids, i)
        at = slice(256 * i, 256 * i + 256)
        for k1 in range(2):
            mixed[128 * k1 : 128 * k1 + 128, at] = x_all[s, 2 * k1 + k2]
        part = dot(mixed[:, at], weights[i][2], 1, 0)
        acc[...] = part if i == 0 else acc[...] + part
    send[...] = acc[...].astype(BF16)


def activations(mine, recv):
    tail = mine[256:257].astype(F32) + recv[256:257].astype(F32)
    total = jnp.concatenate([tail[:, :128] + tail[:, 256:384], tail[:, 128:256] + tail[:, 384:512]])
    cols = [jnp.broadcast_to(total[k : k + 1], (128, 128)).T[:, 0:1] for k in range(2)]
    inv_rms = lax.rsqrt(jnp.concatenate(cols) / 4096 + norm_epsilon)
    pre = (mine[:256].astype(F32) + recv[:256].astype(F32)) * inv_rms
    gate, up = pre[:, :384], pre[:, 384:]
    root = 0.7978845608028654
    tanh = jnp.tanh(root * (gate + 0.044715 * (gate * gate * gate)))
    cdf = 0.5 * (1.0 + tanh)
    slope = cdf + 0.5 * gate * (1.0 - tanh * tanh) * root * (1.0 + 3 * 0.044715 * (gate * gate))
    return inv_rms, gate, up, gate * cdf, slope


def scatter_blocks(ids, held, value):
    for i in range(8):
        _, s, k2 = block_place(ids, i)
        block = value(i).astype(BF16)
        held[s, k2] = block[:128]
        held[s, 2 + k2] = block[128:]


def forward_outputs_kernel(ids, mine, recv, *refs):
    weights, inner, outs, held = refs[:8], refs[8], refs[9:13], refs[13]
    _, _, up, activated, _ = activations(mine, recv)
    inner[...] = (activated * up).astype(BF16)
    scatter_blocks(ids, held, lambda i: dot(inner[...], weights[i][2], 1, 1))
    for s in range(4):
        outs[s][...] = held[s]


def gradients_kernel(
    ids, mine, recv, d_mine, d_recv, inner, tokens, cot, kept, sent, acts, scale, tail
):
    inv_rms, gate, up, activated, slope = activations(mine, recv)
    d_inner = (d_mine[...].astype(F32) + d_recv[...].astype(F32)) * inv_rms
    d_gate = (d_inner * up * slope).astype(BF16)
    d_up = (d_inner * activated).astype(BF16)
    acts[:, :384] = d_gate
    acts[:, 384:] = d_up
    own = (ids[3] // 2) ^ ids[0]
    picked = jnp.where(own == 0, inv_rms[:128], inv_rms[128:])
    scale[...] = jnp.broadcast_to(picked, (128, 128))
    tau = jnp.sum(d_gate.astype(F32) * gate + d_up.astype(F32) * up, axis=1, keepdims=True)
    for k1 in range(2):
        rows = jnp.broadcast_to(tau[128 * k1 : 128 * k1 + 128], (128, 128)).T[:16]
        head, rest = split_float(rows)
        tail[k1, :, :128] = head.astype(BF16)
        tail[k1, :, 128:] = rest.astype(BF16)
    for cc, out in ((1, sent), (0, kept)):
        for w in range(3):
            right = inner[...] if w == 2 else acts[:, 384 * w : 384 * w + 384]
            source = cot if w == 2 else tokens
            left = source[:, 1024 * cc : 1024 * cc + 1024]
            out[w] = dot(left, right, 0, 0).astype(BF16).reshape(4, 256, 384)


def backward_outputs_kernel(ids, acts, tail, *refs):
    weights, outs, held = refs[:8], refs[8:12], refs[12]

    def feat(i):
        return dot(acts[:, :384], weights[i][0], 1, 1) + dot(acts[:, 384:], weights[i][1], 1, 1)

    scatter_blocks(ids, held, feat)
    for s in range(4):
        outs[s][:, :128] = held[s]
        for k in range(4):
            outs[s][k, 128:] = tail[k // 2]


def core_sum_kernel(ids, kept, recv, *outs):
    for t in range(4):
        outs[t][...] = (kept[:, t].astype(F32) + recv[:, t].astype(F32)).astype(BF16)


def sum_refs(refs, at):
    total = refs[0][at].astype(F32)
    for ref in refs[1:]:
        total = total + ref[at].astype(F32)
    return total


def x_sum_kernel(first, ids, *refs):
    forward, backward, outs = refs[:4], refs[4:8], refs[8:]
    for k in range(2):
        outs[k][:128] = sum_refs(forward, first + k).astype(BF16)
        outs[k][128:256] = sum_refs(backward, (first + k, slice(0, 128))).astype(BF16)
        tail = sum_refs(backward, (first + k, slice(128, 144)))
        head, rest = split_float(tail[:, :128] + tail[:, 128:])
        outs[k][256:, :128] = head.astype(BF16)
        outs[k][256:, 128:] = rest.astype(BF16)


def scatter_x(parts):
    return [parts[0]] + [shift(parts[s], "x", -s) for s in (1, 2, 3)]


def finish_kernel(ids, p0, p1, p2, p3, tokens, cot, gain, scale, mixed_out, d_tokens):
    parts = (p0, p1, p2, p3)
    local = tokens[...].astype(F32)
    mixed_out[...] = (local + sum_refs(parts, slice(0, 128))).astype(BF16)
    tail = sum_refs(parts, slice(256, 272))
    tau = (tail[:, :128] + tail[:, 128:])[0:1]
    tau = jnp.broadcast_to(tau, (128, 128)).T
    coef = (scale[...] * tau * (1.0 / 4096))[:, 0:1]
    feat = sum_refs(parts, slice(128, 256)) * gain[ids[3] * 4 + ids[4]]
    d_tokens[...] = cot[...].astype(F32) + feat - local * coef


def grads_sum_kernel(ids, p0, p1, p2, p3, grad_gate, grad_up, grad_down):
    parts = (p0, p1, p2, p3)
    grad_gate[...] = sum_refs(parts, 0)
    grad_up[...] = sum_refs(parts, 1)
    grad_down[...] = sum_refs(parts, 2).T


def after(value, *events):
    return lax.optimization_barrier((value, *events))[0]


def on_device(tokens, norm_gain, gate_weight, up_weight, down_weight, out_cotangent):
    ids = jnp.stack([lax.axis_index(n) for n in ("zh", "y", "c", "zl", "x")]).astype(jnp.int32)
    gain = norm_gain.reshape(16, 1, 256)

    pair = jnp.stack([tokens, out_cotangent])
    own = jnp.stack([gate_weight, up_weight, down_weight.T])
    by_z = [lax.ppermute(pair, ("zh", "zl"), z_pairs(k)) for k in range(4)]
    tok_z, cot_z = call(stack_kernel, ids, by_z, [VMEM] * 4, [((4, 128, 256), BF16)] * 2)
    y1, y3, *_ = lax.optimization_barrier((shift(own, "y", 1), shift(own, "y", 3), *by_z))
    y2 = shift(after(own, y1, y3), "y", 2)
    tok_x = [shift(tok_z, "x", s) for s in (1, 2, 3)]
    y2 = after(y2, *tok_x)
    cot_z = after(cot_z, *tok_x)
    tok_x = [tok_z] + tok_x
    by_y = [own, y1, y2, y3]
    weights = by_y + [swap(piece, "c") for piece in by_y]

    x_all = pltpu.VMEM((4, 4, 128, 256), BF16)
    send, tok_all = call(
        forward_products_kernel,
        ids,
        [*tok_x, *weights, gain],
        [VMEM] * 13,
        [((272, 768), BF16), ((256, 2048), BF16)],
        [x_all, pltpu.VMEM((256, 768), F32)],
    )
    cot_x = [cot_z] + [shift(cot_z, "x", s) for s in (1, 2, 3)]
    d_send, cot_all = call(
        backward_products_kernel,
        ids,
        [*cot_x, *weights],
        [VMEM] * 12,
        [((256, 384), BF16), ((256, 2048), BF16)],
        [x_all, pltpu.VMEM((256, 384), F32)],
    )
    recv = swap(send, "zh")
    held = pltpu.VMEM((4, 4, 128, 256), BF16)
    inner, *forward = call(
        forward_outputs_kernel,
        ids,
        [after(send, d_send), recv, *weights],
        [VMEM] * 10,
        [((256, 384), BF16)] + [((4, 128, 256), BF16)] * 4,
        [held],
        8,
        1 << 29,
    )
    forward = scatter_x(forward)
    inner = after(inner, *forward[1:])
    kept, sent, acts, scale, tail = call(
        gradients_kernel,
        ids,
        [send, recv, d_send, swap(d_send, "zh"), inner, tok_all, cot_all],
        [VMEM] * 7,
        [((3, 4, 256, 384), BF16)] * 2
        + [((256, 768), BF16), ((128, 128), F32), ((2, 16, 256), BF16)],
        (),
        16,
        1 << 31,
    )
    backward = call(
        backward_outputs_kernel,
        ids,
        [acts, tail, *weights],
        [VMEM] * 10,
        [((4, 144, 256), BF16)] * 4,
        [held],
        8,
        1 << 30,
    )
    backward = scatter_x(backward)
    sums = list(
        call(core_sum_kernel, ids, [kept, swap(sent, "c")], [VMEM] * 2, [((3, 256, 384), BF16)] * 4)
    )
    near = [shift(sums[1], "y", -1), shift(sums[3], "y", 1)]
    blocks = []
    for k in (0, 2):
        body = functools.partial(x_sum_kernel, k)
        parts = [*forward, *backward]
        blocks += call(body, ids, parts, [VMEM] * 8, [((272, 256), BF16)] * 2)
    blocks[2:] = [after(blocks[2], near[0]), after(blocks[3], near[1])]
    far = shift(after(sums[2], blocks[0]), "y", 2)
    blocks = [
        lax.ppermute(blocks[k], ("zh", "zl"), [(t, s) for s, t in z_pairs(k)]) for k in range(4)
    ]
    grad_gate, grad_up, grad_down = call(
        grads_sum_kernel,
        ids,
        [sums[0], near[0], far, near[1]],
        [VMEM] * 4,
        [((256, 384), F32), ((256, 384), F32), ((384, 256), F32)],
        (),
        16,
    )
    scale = after(scale, grad_gate)
    mixed_out, d_tokens = call(
        finish_kernel,
        ids,
        [*blocks, tokens, out_cotangent, gain, scale],
        [VMEM] * 8,
        [((128, 256), BF16), ((128, 256), F32)],
    )
    return (mixed_out, d_tokens, grad_gate, grad_up, grad_down)


def solution(mesh):
    split = Mesh(mesh.devices.reshape(2, 4, 2, 4, 4), ("zh", "y", "c", "zl", "x"))
    grp, dev = ("zh", "y", "c"), ("zl", "x")
    in_specs = (P(grp, dev), P(), P(grp, dev), P(grp, dev), P(dev, grp), P(grp, dev))
    out_specs = (P(grp, dev), P(grp, dev), P(grp, dev), P(grp, dev), P(dev, grp))
    return jax.shard_map(
        on_device, mesh=split, in_specs=in_specs, out_specs=out_specs, check_vma=False
    )
```

```python
import functools
import math

import jax
import jax.numpy as jnp
from jax import lax
from jax.experimental import pallas as pl
from jax.experimental.pallas import tpu as pltpu
from jax.sharding import Mesh
from jax.sharding import PartitionSpec as P

norm_epsilon = 1e-06
F32 = jnp.float32
BF16 = jnp.bfloat16
SMEM = pl.BlockSpec(memory_space=pltpu.SMEM)
VMEM = pl.BlockSpec(memory_space=pltpu.VMEM)
MIB = 1 << 20


def dot(left, right, left_dim, right_dim):
    return lax.dot_general(
        left, right, (((left_dim,), (right_dim,)), ((), ())), preferred_element_type=F32
    )


def shift(array, axis, by):
    return lax.ppermute(array, axis, [(i, (i + by) % 4) for i in range(4)])


def swap(array, axis):
    return lax.ppermute(array, axis, [(0, 1), (1, 0)])


def z_pairs(k):
    k1, k2 = k // 2, k % 2
    return [
        (4 * zs + 2 * h + l, 4 * h + 2 * (zs ^ k1) + (l ^ k2))
        for zs in range(2)
        for h in range(2)
        for l in range(2)
    ]


def split_float(value):
    head = value.astype(BF16).astype(F32)
    return head, value - head


def call(body, ids, operands, specs, outs, scratch=(), limit=8, flops=0):
    size = sum(a.size * a.dtype.itemsize for a in operands)
    size += sum(2 * math.prod(shape) for shape, _ in outs)
    return pl.pallas_call(
        body,
        out_shape=[jax.ShapeDtypeStruct(s, d) for s, d in outs],
        in_specs=[SMEM] + specs,
        out_specs=[VMEM] * len(outs),
        scratch_shapes=list(scratch),
        compiler_params=pltpu.CompilerParams(vmem_limit_bytes=limit * MIB),
        cost_estimate=pl.CostEstimate(flops=flops, bytes_accessed=size, transcendentals=0),
    )(ids, *operands)


def block_place(ids, i):
    q = lax.rem(ids[1] - i % 4 + 4, 4) * 2 + (ids[2] ^ (i // 4))
    return q, lax.rem(ids[4] - lax.rem(q, 4) + 4, 4), (ids[3] % 2) ^ (q // 4)


def stack_kernel(ids, p0, p1, p2, p3, tokens, cot):
    for k, piece in enumerate((p0, p1, p2, p3)):
        tokens[k] = piece[0]
        cot[k] = piece[1]


def forward_products_kernel(ids, *refs):
    pieces, weights, (gain, send, mixed, x_all, acc) = refs[:4], refs[4:12], refs[12:]
    for s in range(4):
        x_all[s] = pieces[s][...]
    total = [jnp.zeros((128, 1), F32) for _ in range(2)]
    for i in range(8):
        q, s, k2 = block_place(ids, i)
        row = gain[ids[0] * 8 + q]
        at = slice(256 * i, 256 * i + 256)
        for k1 in range(2):
            value = x_all[s, 2 * k1 + k2].astype(F32)
            total[k1] = total[k1] + jnp.sum(value * value, axis=1, keepdims=True)
            mixed[128 * k1 : 128 * k1 + 128, at] = (value * row).astype(BF16)
        for w in range(2):
            part = dot(mixed[:, at], weights[i][w], 1, 0)
            cols = slice(384 * w, 384 * w + 384)
            acc[:, cols] = part if i == 0 else acc[:, cols] + part
    send[:256] = acc[...].astype(BF16)
    send[256:, :] = jnp.zeros((16, 768), BF16)
    for k1 in range(2):
        head, rest = split_float(jnp.broadcast_to(total[k1], (128, 128)).T[:16])
        send[256:, 128 * k1 : 128 * k1 + 128] = head.astype(BF16)
        send[256:, 256 + 128 * k1 : 384 + 128 * k1] = rest.astype(BF16)


def backward_products_kernel(ids, *refs):
    pieces, weights, (send, mixed, x_all, acc) = refs[:4], refs[4:12], refs[12:]
    for s in range(4):
        x_all[s] = pieces[s][...]
    for i in range(8):
        _, s, k2 = block_place(ids, i)
        at = slice(256 * i, 256 * i + 256)
        for k1 in range(2):
            mixed[128 * k1 : 128 * k1 + 128, at] = x_all[s, 2 * k1 + k2]
        part = dot(mixed[:, at], weights[i][2], 1, 0)
        acc[...] = part if i == 0 else acc[...] + part
    send[...] = acc[...].astype(BF16)


def activations(mine, recv):
    tail = mine[256:257].astype(F32) + recv[256:257].astype(F32)
    total = jnp.concatenate([tail[:, :128] + tail[:, 256:384], tail[:, 128:256] + tail[:, 384:512]])
    cols = [jnp.broadcast_to(total[k : k + 1], (128, 128)).T[:, 0:1] for k in range(2)]
    inv_rms = lax.rsqrt(jnp.concatenate(cols) / 4096 + norm_epsilon)
    pre = (mine[:256].astype(F32) + recv[:256].astype(F32)) * inv_rms
    gate, up = pre[:, :384], pre[:, 384:]
    root = 0.7978845608028654
    tanh = jnp.tanh(root * (gate + 0.044715 * (gate * gate * gate)))
    cdf = 0.5 * (1.0 + tanh)
    slope = cdf + 0.5 * gate * (1.0 - tanh * tanh) * root * (1.0 + 3 * 0.044715 * (gate * gate))
    return inv_rms, gate, up, gate * cdf, slope


def scatter_blocks(ids, held, value):
    for i in range(8):
        _, s, k2 = block_place(ids, i)
        block = value(i).astype(BF16)
        held[s, k2] = block[:128]
        held[s, 2 + k2] = block[128:]


def forward_outputs_kernel(ids, mine, recv, *refs):
    weights, inner, outs, held = refs[:8], refs[8], refs[9:13], refs[13]
    _, _, up, activated, _ = activations(mine, recv)
    inner[...] = (activated * up).astype(BF16)
    scatter_blocks(ids, held, lambda i: dot(inner[...], weights[i][2], 1, 1))
    for s in range(4):
        outs[s][...] = held[s]


def elementwise_kernel(ids, mine, recv, d_mine, d_recv, acts, scale, tail):
    inv_rms, gate, up, activated, slope = activations(mine, recv)
    d_inner = (d_mine[...].astype(F32) + d_recv[...].astype(F32)) * inv_rms
    d_gate = (d_inner * up * slope).astype(BF16)
    d_up = (d_inner * activated).astype(BF16)
    acts[:, :384] = d_gate
    acts[:, 384:] = d_up
    own = (ids[3] // 2) ^ ids[0]
    picked = jnp.where(own == 0, inv_rms[:128], inv_rms[128:])
    scale[...] = jnp.broadcast_to(picked, (128, 128))
    tau = jnp.sum(d_gate.astype(F32) * gate + d_up.astype(F32) * up, axis=1, keepdims=True)
    for k1 in range(2):
        rows = jnp.broadcast_to(tau[128 * k1 : 128 * k1 + 128], (128, 128)).T[:16]
        head, rest = split_float(rows)
        tail[k1, :, :128] = head.astype(BF16)
        tail[k1, :, 128:] = rest.astype(BF16)


def gradients_kernel(ids, acts, inner, tokens, cot, kept, sent):
    for cc, out in ((1, sent), (0, kept)):
        for w in range(3):
            right = inner[...] if w == 2 else acts[:, 384 * w : 384 * w + 384]
            source = cot if w == 2 else tokens
            left = source[:, 1024 * cc : 1024 * cc + 1024]
            out[w] = dot(left, right, 0, 0).astype(BF16).reshape(4, 256, 384)


def backward_outputs_kernel(ids, acts, tail, *refs):
    weights, outs, held = refs[:8], refs[8:12], refs[12]

    def feat(i):
        return dot(acts[:, :384], weights[i][0], 1, 1) + dot(acts[:, 384:], weights[i][1], 1, 1)

    scatter_blocks(ids, held, feat)
    for s in range(4):
        outs[s][:, :128] = held[s]
        for k in range(4):
            outs[s][k, 128:] = tail[k // 2]


def core_sum_kernel(ids, kept, recv, *outs):
    for t in range(4):
        outs[t][...] = (kept[:, t].astype(F32) + recv[:, t].astype(F32)).astype(BF16)


def sum_refs(refs, at):
    total = refs[0][at].astype(F32)
    for ref in refs[1:]:
        total = total + ref[at].astype(F32)
    return total


def x_sum_kernel(first, ids, *refs):
    forward, backward, outs = refs[:4], refs[4:8], refs[8:]
    for k in range(2):
        outs[k][:128] = sum_refs(forward, first + k).astype(BF16)
        outs[k][128:256] = sum_refs(backward, (first + k, slice(0, 128))).astype(BF16)
        tail = sum_refs(backward, (first + k, slice(128, 144)))
        head, rest = split_float(tail[:, :128] + tail[:, 128:])
        outs[k][256:, :128] = head.astype(BF16)
        outs[k][256:, 128:] = rest.astype(BF16)


def scatter_x(parts):
    return [parts[0]] + [shift(parts[s], "x", -s) for s in (1, 2, 3)]


def finish_kernel(ids, p0, p1, p2, p3, tokens, cot, gain, scale, mixed_out, d_tokens):
    parts = (p0, p1, p2, p3)
    local = tokens[...].astype(F32)
    mixed_out[...] = (local + sum_refs(parts, slice(0, 128))).astype(BF16)
    tail = sum_refs(parts, slice(256, 272))
    tau = (tail[:, :128] + tail[:, 128:])[0:1]
    tau = jnp.broadcast_to(tau, (128, 128)).T
    coef = (scale[...] * tau * (1.0 / 4096))[:, 0:1]
    feat = sum_refs(parts, slice(128, 256)) * gain[ids[3] * 4 + ids[4]]
    d_tokens[...] = cot[...].astype(F32) + feat - local * coef


def grads_sum_kernel(ids, p0, p1, p2, p3, grad_gate, grad_up, grad_down):
    parts = (p0, p1, p2, p3)
    grad_gate[...] = sum_refs(parts, 0)
    grad_up[...] = sum_refs(parts, 1)
    grad_down[...] = sum_refs(parts, 2).T


def after(value, *events):
    return lax.optimization_barrier((value, *events))[0]


def on_device(tokens, norm_gain, gate_weight, up_weight, down_weight, out_cotangent):
    ids = jnp.stack([lax.axis_index(n) for n in ("zh", "y", "c", "zl", "x")]).astype(jnp.int32)
    gain = norm_gain.reshape(16, 1, 256)

    pair = jnp.stack([tokens, out_cotangent])
    own = jnp.stack([gate_weight, up_weight, down_weight.T])
    by_z = [lax.ppermute(pair, ("zh", "zl"), z_pairs(k)) for k in range(4)]
    tok_z, cot_z = call(stack_kernel, ids, by_z, [VMEM] * 4, [((4, 128, 256), BF16)] * 2)
    y1, y3, *_ = lax.optimization_barrier((shift(own, "y", 1), shift(own, "y", 3), *by_z))
    y2 = shift(after(own, y1, y3), "y", 2)
    tok_x = [shift(tok_z, "x", s) for s in (1, 2, 3)]
    y2 = after(y2, *tok_x)
    cot_z = after(cot_z, *tok_x)
    tok_x = [tok_z] + tok_x
    by_y = [own, y1, y2, y3]
    weights = by_y + [swap(piece, "c") for piece in by_y]

    x_all = pltpu.VMEM((4, 4, 128, 256), BF16)
    send, tok_all = call(
        forward_products_kernel,
        ids,
        [*tok_x, *weights, gain],
        [VMEM] * 13,
        [((272, 768), BF16), ((256, 2048), BF16)],
        [x_all, pltpu.VMEM((256, 768), F32)],
    )
    cot_x = [cot_z] + [shift(cot_z, "x", s) for s in (1, 2, 3)]
    d_send, cot_all = call(
        backward_products_kernel,
        ids,
        [*cot_x, *weights],
        [VMEM] * 12,
        [((256, 384), BF16), ((256, 2048), BF16)],
        [x_all, pltpu.VMEM((256, 384), F32)],
    )
    recv = swap(send, "zh")
    held = pltpu.VMEM((4, 4, 128, 256), BF16)
    inner, *forward = call(
        forward_outputs_kernel,
        ids,
        [after(send, d_send), recv, *weights],
        [VMEM] * 10,
        [((256, 384), BF16)] + [((4, 128, 256), BF16)] * 4,
        [held],
        8,
        1 << 29,
    )
    forward = scatter_x(forward)
    acts, scale, tail = call(
        elementwise_kernel,
        ids,
        [send, recv, d_send, swap(d_send, "zh")],
        [VMEM] * 4,
        [((256, 768), BF16), ((128, 128), F32), ((2, 16, 256), BF16)],
    )
    backward = call(
        backward_outputs_kernel,
        ids,
        [acts, tail, *weights],
        [VMEM] * 10,
        [((4, 144, 256), BF16)] * 4,
        [held],
        8,
        1 << 30,
    )
    kept, sent = call(
        gradients_kernel,
        ids,
        [acts, after(inner, *forward[1:], backward[0]), tok_all, cot_all],
        [VMEM] * 4,
        [((3, 4, 256, 384), BF16)] * 2,
        (),
        16,
        1 << 31,
    )
    backward = scatter_x(backward)
    sums = list(
        call(core_sum_kernel, ids, [kept, swap(sent, "c")], [VMEM] * 2, [((3, 256, 384), BF16)] * 4)
    )
    near = [shift(sums[1], "y", -1), shift(sums[3], "y", 1)]
    blocks = []
    for k in (0, 2):
        body = functools.partial(x_sum_kernel, k)
        parts = [*forward, *backward]
        blocks += call(body, ids, parts, [VMEM] * 8, [((272, 256), BF16)] * 2)
    blocks[2:] = [after(blocks[2], near[0]), after(blocks[3], near[1])]
    far = shift(after(sums[2], blocks[0]), "y", 2)
    blocks = [
        lax.ppermute(blocks[k], ("zh", "zl"), [(t, s) for s, t in z_pairs(k)]) for k in range(4)
    ]
    grad_gate, grad_up, grad_down = call(
        grads_sum_kernel,
        ids,
        [sums[0], near[0], far, near[1]],
        [VMEM] * 4,
        [((256, 384), F32), ((256, 384), F32), ((384, 256), F32)],
        (),
        16,
    )
    scale = after(scale, grad_gate)
    mixed_out, d_tokens = call(
        finish_kernel,
        ids,
        [*blocks, tokens, out_cotangent, gain, scale],
        [VMEM] * 8,
        [((128, 256), BF16), ((128, 256), F32)],
    )
    return (mixed_out, d_tokens, grad_gate, grad_up, grad_down)


def solution(mesh):
    split = Mesh(mesh.devices.reshape(2, 4, 2, 4, 4), ("zh", "y", "c", "zl", "x"))
    grp, dev = ("zh", "y", "c"), ("zl", "x")
    in_specs = (P(grp, dev), P(), P(grp, dev), P(grp, dev), P(dev, grp), P(grp, dev))
    out_specs = (P(grp, dev), P(grp, dev), P(grp, dev), P(grp, dev), P(dev, grp))
    return jax.shard_map(
        on_device, mesh=split, in_specs=in_specs, out_specs=out_specs, check_vma=False
    )
```

```python
import functools
import math

import jax
import jax.numpy as jnp
from jax import lax
from jax.experimental import pallas as pl
from jax.experimental.pallas import tpu as pltpu
from jax.sharding import Mesh
from jax.sharding import PartitionSpec as P

norm_epsilon = 1e-06
F32 = jnp.float32
BF16 = jnp.bfloat16
SMEM = pl.BlockSpec(memory_space=pltpu.SMEM)
VMEM = pl.BlockSpec(memory_space=pltpu.VMEM)
MIB = 1 << 20


def dot(left, right, left_dim, right_dim):
    return lax.dot_general(
        left, right, (((left_dim,), (right_dim,)), ((), ())), preferred_element_type=F32
    )


def shift(array, axis, by):
    return lax.ppermute(array, axis, [(i, (i + by) % 4) for i in range(4)])


def swap(array, axis):
    return lax.ppermute(array, axis, [(0, 1), (1, 0)])


def z_pairs(k):
    k1, k2 = k // 2, k % 2
    return [
        (4 * zs + 2 * h + l, 4 * h + 2 * (zs ^ k1) + (l ^ k2))
        for zs in range(2)
        for h in range(2)
        for l in range(2)
    ]


def split_float(value):
    head = value.astype(BF16).astype(F32)
    return head, value - head


def call(body, ids, operands, specs, outs, scratch=(), limit=8, flops=0):
    size = sum(a.size * a.dtype.itemsize for a in operands)
    size += sum(2 * math.prod(shape) for shape, _ in outs)
    return pl.pallas_call(
        body,
        out_shape=[jax.ShapeDtypeStruct(s, d) for s, d in outs],
        in_specs=[SMEM] + specs,
        out_specs=[VMEM] * len(outs),
        scratch_shapes=list(scratch),
        compiler_params=pltpu.CompilerParams(vmem_limit_bytes=limit * MIB),
        cost_estimate=pl.CostEstimate(flops=flops, bytes_accessed=size, transcendentals=0),
    )(ids, *operands)


def block_place(ids, i):
    q = lax.rem(ids[1] - i % 4 + 4, 4) * 2 + (ids[2] ^ (i // 4))
    return q, lax.rem(ids[4] - lax.rem(q, 4) + 4, 4), (ids[3] % 2) ^ (q // 4)


def stack_kernel(ids, p0, p2, p3, p1, tokens, cot):
    for k, piece in enumerate((p0, p1, p2, p3)):
        tokens[k] = piece[0]
        cot[k] = piece[1]


def forward_products_kernel(ids, *refs):
    pieces, weights, (gain, send, mixed, x_all, acc) = refs[:4], refs[4:12], refs[12:]
    for s in range(4):
        x_all[s] = pieces[s][...]
    total = [jnp.zeros((128, 1), F32) for _ in range(2)]
    for i in range(8):
        q, s, k2 = block_place(ids, i)
        row = gain[ids[0] * 8 + q]
        at = slice(256 * i, 256 * i + 256)
        for k1 in range(2):
            value = x_all[s, 2 * k1 + k2].astype(F32)
            total[k1] = total[k1] + jnp.sum(value * value, axis=1, keepdims=True)
            mixed[128 * k1 : 128 * k1 + 128, at] = (value * row).astype(BF16)
        for w in range(2):
            part = dot(mixed[:, at], weights[i][w], 1, 0)
            cols = slice(384 * w, 384 * w + 384)
            acc[:, cols] = part if i == 0 else acc[:, cols] + part
    send[:256] = acc[...].astype(BF16)
    send[256:, :] = jnp.zeros((16, 768), BF16)
    for k1 in range(2):
        head, rest = split_float(jnp.broadcast_to(total[k1], (128, 128)).T[:16])
        send[256:, 128 * k1 : 128 * k1 + 128] = head.astype(BF16)
        send[256:, 256 + 128 * k1 : 384 + 128 * k1] = rest.astype(BF16)


def backward_products_kernel(ids, *refs):
    pieces, weights, (send, mixed, x_all, acc) = refs[:4], refs[4:12], refs[12:]
    for s in range(4):
        x_all[s] = pieces[s][...]
    for i in range(8):
        _, s, k2 = block_place(ids, i)
        at = slice(256 * i, 256 * i + 256)
        for k1 in range(2):
            mixed[128 * k1 : 128 * k1 + 128, at] = x_all[s, 2 * k1 + k2]
        part = dot(mixed[:, at], weights[i][2], 1, 0)
        acc[...] = part if i == 0 else acc[...] + part
    send[...] = acc[...].astype(BF16)


def activations(mine, recv):
    tail = mine[256:257].astype(F32) + recv[256:257].astype(F32)
    total = jnp.concatenate([tail[:, :128] + tail[:, 256:384], tail[:, 128:256] + tail[:, 384:512]])
    cols = [jnp.broadcast_to(total[k : k + 1], (128, 128)).T[:, 0:1] for k in range(2)]
    inv_rms = lax.rsqrt(jnp.concatenate(cols) / 4096 + norm_epsilon)
    pre = (mine[:256].astype(F32) + recv[:256].astype(F32)) * inv_rms
    gate, up = pre[:, :384], pre[:, 384:]
    root = 0.7978845608028654
    tanh = jnp.tanh(root * (gate + 0.044715 * (gate * gate * gate)))
    cdf = 0.5 * (1.0 + tanh)
    slope = cdf + 0.5 * gate * (1.0 - tanh * tanh) * root * (1.0 + 3 * 0.044715 * (gate * gate))
    return inv_rms, gate, up, gate * cdf, slope


def scatter_blocks(ids, held, value):
    for i in range(8):
        _, s, k2 = block_place(ids, i)
        block = value(i).astype(BF16)
        held[s, k2] = block[:128]
        held[s, 2 + k2] = block[128:]


def forward_outputs_kernel(ids, mine, recv, *refs):
    weights, inner, outs, held = refs[:8], refs[8], refs[9:13], refs[13]
    _, _, up, activated, _ = activations(mine, recv)
    inner[...] = (activated * up).astype(BF16)
    scatter_blocks(ids, held, lambda i: dot(inner[...], weights[i][2], 1, 1))
    for s in range(4):
        outs[s][...] = held[s]


def elementwise_kernel(ids, mine, recv, d_mine, d_recv, acts, scale, tail):
    inv_rms, gate, up, activated, slope = activations(mine, recv)
    d_inner = (d_mine[...].astype(F32) + d_recv[...].astype(F32)) * inv_rms
    d_gate = (d_inner * up * slope).astype(BF16)
    d_up = (d_inner * activated).astype(BF16)
    acts[:, :384] = d_gate
    acts[:, 384:] = d_up
    own = (ids[3] // 2) ^ ids[0]
    picked = jnp.where(own == 0, inv_rms[:128], inv_rms[128:])
    scale[...] = jnp.broadcast_to(picked, (128, 128))
    tau = jnp.sum(d_gate.astype(F32) * gate + d_up.astype(F32) * up, axis=1, keepdims=True)
    for k1 in range(2):
        rows = jnp.broadcast_to(tau[128 * k1 : 128 * k1 + 128], (128, 128)).T[:16]
        head, rest = split_float(rows)
        tail[k1, :, :128] = head.astype(BF16)
        tail[k1, :, 128:] = rest.astype(BF16)


def gradients_kernel(ids, acts, inner, tokens, cot, kept, sent):
    for cc, out in ((1, sent), (0, kept)):
        for w in range(3):
            right = inner[...] if w == 2 else acts[:, 384 * w : 384 * w + 384]
            source = cot if w == 2 else tokens
            left = source[:, 1024 * cc : 1024 * cc + 1024]
            out[w] = dot(left, right, 0, 0).astype(BF16).reshape(4, 256, 384)


def backward_outputs_kernel(ids, acts, tail, *refs):
    weights, outs, held = refs[:8], refs[8:12], refs[12]

    def feat(i):
        return dot(acts[:, :384], weights[i][0], 1, 1) + dot(acts[:, 384:], weights[i][1], 1, 1)

    scatter_blocks(ids, held, feat)
    for s in range(4):
        outs[s][:, :128] = held[s]
        for k in range(4):
            outs[s][k, 128:] = tail[k // 2]


def core_sum_kernel(ids, kept, recv, *outs):
    for t in range(4):
        outs[t][...] = (kept[:, t].astype(F32) + recv[:, t].astype(F32)).astype(BF16)


def sum_refs(refs, at):
    total = refs[0][at].astype(F32)
    for ref in refs[1:]:
        total = total + ref[at].astype(F32)
    return total


def x_sum_kernel(first, ids, *refs):
    forward, backward, outs = refs[:4], refs[4:8], refs[8:]
    for k in range(2):
        outs[k][:128] = sum_refs(forward, first + k).astype(BF16)
        outs[k][128:256] = sum_refs(backward, (first + k, slice(0, 128))).astype(BF16)
        tail = sum_refs(backward, (first + k, slice(128, 144)))
        head, rest = split_float(tail[:, :128] + tail[:, 128:])
        outs[k][256:, :128] = head.astype(BF16)
        outs[k][256:, 128:] = rest.astype(BF16)


def scatter_x(parts):
    return [parts[0]] + [shift(parts[s], "x", -s) for s in (1, 2, 3)]


def finish_kernel(ids, p0, p1, p2, p3, tokens, cot, gain, scale, mixed_out, d_tokens):
    parts = (p0, p1, p2, p3)
    local = tokens[...].astype(F32)
    mixed_out[...] = (local + sum_refs(parts, slice(0, 128))).astype(BF16)
    tail = sum_refs(parts, slice(256, 272))
    tau = (tail[:, :128] + tail[:, 128:])[0:1]
    tau = jnp.broadcast_to(tau, (128, 128)).T
    coef = (scale[...] * tau * (1.0 / 4096))[:, 0:1]
    feat = sum_refs(parts, slice(128, 256)) * gain[ids[3] * 4 + ids[4]]
    d_tokens[...] = cot[...].astype(F32) + feat - local * coef


def grads_sum_kernel(ids, p0, p1, p2, p3, grad_gate, grad_up, grad_down):
    parts = (p0, p1, p2, p3)
    grad_gate[...] = sum_refs(parts, 0)
    grad_up[...] = sum_refs(parts, 1)
    grad_down[...] = sum_refs(parts, 2).T


def after(value, *events):
    return lax.optimization_barrier((value, *events))[0]


def on_device(tokens, norm_gain, gate_weight, up_weight, down_weight, out_cotangent):
    ids = jnp.stack([lax.axis_index(n) for n in ("zh", "y", "c", "zl", "x")]).astype(jnp.int32)
    gain = norm_gain.reshape(16, 1, 256)

    pair = jnp.stack([tokens, out_cotangent])
    own = jnp.stack([gate_weight, up_weight, down_weight.T])
    by_z = [lax.ppermute(pair, ("zh", "zl"), z_pairs(k)) for k in range(4)]
    tok_z, cot_z = call(stack_kernel, ids, [by_z[k] for k in (0, 2, 3, 1)], [VMEM] * 4, [((4, 128, 256), BF16)] * 2)
    y1, y3, *_ = lax.optimization_barrier((shift(own, "y", 1), shift(own, "y", 3), *[by_z[k] for k in (0, 2, 3, 1)]))
    y2 = shift(after(own, y1, y3), "y", 2)
    tok_x = [shift(tok_z, "x", s) for s in (1, 2, 3)]
    y2 = after(y2, *tok_x)
    cot_z = after(cot_z, *tok_x)
    tok_x = [tok_z] + tok_x
    by_y = [own, y1, y2, y3]
    weights = by_y + [swap(piece, "c") for piece in by_y]

    x_all = pltpu.VMEM((4, 4, 128, 256), BF16)
    send, tok_all = call(
        forward_products_kernel,
        ids,
        [*tok_x, *weights, gain],
        [VMEM] * 13,
        [((272, 768), BF16), ((256, 2048), BF16)],
        [x_all, pltpu.VMEM((256, 768), F32)],
    )
    cot_x = [cot_z] + [shift(cot_z, "x", s) for s in (1, 2, 3)]
    d_send, cot_all = call(
        backward_products_kernel,
        ids,
        [*cot_x, *weights],
        [VMEM] * 12,
        [((256, 384), BF16), ((256, 2048), BF16)],
        [x_all, pltpu.VMEM((256, 384), F32)],
    )
    recv = swap(send, "zh")
    held = pltpu.VMEM((4, 4, 128, 256), BF16)
    inner, *forward = call(
        forward_outputs_kernel,
        ids,
        [after(send, d_send), recv, *weights],
        [VMEM] * 10,
        [((256, 384), BF16)] + [((4, 128, 256), BF16)] * 4,
        [held],
        8,
        1 << 29,
    )
    forward = scatter_x(forward)
    acts, scale, tail = call(
        elementwise_kernel,
        ids,
        [send, recv, d_send, swap(d_send, "zh")],
        [VMEM] * 4,
        [((256, 768), BF16), ((128, 128), F32), ((2, 16, 256), BF16)],
    )
    backward = call(
        backward_outputs_kernel,
        ids,
        [acts, tail, *weights],
        [VMEM] * 10,
        [((4, 144, 256), BF16)] * 4,
        [held],
        8,
        1 << 30,
    )
    kept, sent = call(
        gradients_kernel,
        ids,
        [acts, after(inner, *forward[1:], backward[0]), tok_all, cot_all],
        [VMEM] * 4,
        [((3, 4, 256, 384), BF16)] * 2,
        (),
        16,
        1 << 31,
    )
    backward = scatter_x(backward)
    sums = list(
        call(core_sum_kernel, ids, [kept, swap(sent, "c")], [VMEM] * 2, [((3, 256, 384), BF16)] * 4)
    )
    near = [shift(sums[1], "y", -1), shift(sums[3], "y", 1)]
    blocks = []
    for k in (0, 2):
        body = functools.partial(x_sum_kernel, k)
        parts = [*forward, *backward]
        blocks += call(body, ids, parts, [VMEM] * 8, [((272, 256), BF16)] * 2)
    blocks[3] = after(blocks[3], *near)
    far = shift(after(sums[2], blocks[2]), "y", 2)
    blocks = [
        lax.ppermute(blocks[k], ("zh", "zl"), [(t, s) for s, t in z_pairs(k)]) for k in range(4)
    ]
    grad_gate, grad_up, grad_down = call(
        grads_sum_kernel,
        ids,
        [sums[0], near[0], far, near[1]],
        [VMEM] * 4,
        [((256, 384), F32), ((256, 384), F32), ((384, 256), F32)],
        (),
        16,
    )
    scale = after(scale, grad_gate)
    mixed_out, d_tokens = call(
        finish_kernel,
        ids,
        [*blocks, tokens, out_cotangent, gain, scale],
        [VMEM] * 8,
        [((128, 256), BF16), ((128, 256), F32)],
    )
    return (mixed_out, d_tokens, grad_gate, grad_up, grad_down)


def solution(mesh):
    split = Mesh(mesh.devices.reshape(2, 4, 2, 4, 4), ("zh", "y", "c", "zl", "x"))
    grp, dev = ("zh", "y", "c"), ("zl", "x")
    in_specs = (P(grp, dev), P(), P(grp, dev), P(grp, dev), P(dev, grp), P(grp, dev))
    out_specs = (P(grp, dev), P(grp, dev), P(grp, dev), P(grp, dev), P(dev, grp))
    return jax.shard_map(
        on_device, mesh=split, in_specs=in_specs, out_specs=out_specs, check_vma=False
    )
```

```python
import functools
import math

import jax
import jax.numpy as jnp
from jax import lax
from jax.experimental import pallas as pl
from jax.experimental.pallas import tpu as pltpu
from jax.sharding import Mesh
from jax.sharding import PartitionSpec as P

norm_epsilon = 1e-06
F32 = jnp.float32
BF16 = jnp.bfloat16
SMEM = pl.BlockSpec(memory_space=pltpu.SMEM)
VMEM = pl.BlockSpec(memory_space=pltpu.VMEM)
MIB = 1 << 20


def dot(left, right, left_dim, right_dim):
    return lax.dot_general(
        left, right, (((left_dim,), (right_dim,)), ((), ())), preferred_element_type=F32
    )


def shift(array, axis, by):
    return lax.ppermute(array, axis, [(i, (i + by) % 4) for i in range(4)])


def swap(array, axis):
    return lax.ppermute(array, axis, [(0, 1), (1, 0)])


def z_pairs(k):
    k1, k2 = k // 2, k % 2
    return [
        (4 * zs + 2 * h + l, 4 * h + 2 * (zs ^ k1) + (l ^ k2))
        for zs in range(2)
        for h in range(2)
        for l in range(2)
    ]


def split_float(value):
    head = value.astype(BF16).astype(F32)
    return head, value - head


def call(body, ids, operands, specs, outs, scratch=(), limit=8, flops=0):
    size = sum(a.size * a.dtype.itemsize for a in operands)
    size += sum(2 * math.prod(shape) for shape, _ in outs)
    return pl.pallas_call(
        body,
        out_shape=[jax.ShapeDtypeStruct(s, d) for s, d in outs],
        in_specs=[SMEM] + specs,
        out_specs=[VMEM] * len(outs),
        scratch_shapes=list(scratch),
        compiler_params=pltpu.CompilerParams(vmem_limit_bytes=limit * MIB),
        cost_estimate=pl.CostEstimate(flops=flops, bytes_accessed=size, transcendentals=0),
    )(ids, *operands)


def block_place(ids, i):
    q = lax.rem(ids[1] - i % 4 + 4, 4) * 2 + (ids[2] ^ (i // 4))
    return q, lax.rem(ids[4] - lax.rem(q, 4) + 4, 4), (ids[3] % 2) ^ (q // 4)


def stack_kernel(ids, p0, p2, p3, p1, tokens, cot):
    for k, piece in enumerate((p0, p1, p2, p3)):
        tokens[k] = piece[0]
        cot[k] = piece[1]


def forward_products_kernel(ids, *refs):
    pieces, weights, (gain, send, mixed, x_all, acc) = refs[:4], refs[4:12], refs[12:]
    for j, s in enumerate((0, 1, 3, 2)):
        x_all[s] = pieces[j][...]
    total = [jnp.zeros((128, 1), F32) for _ in range(2)]
    for i in range(8):
        q, s, k2 = block_place(ids, i)
        row = gain[ids[0] * 8 + q]
        at = slice(256 * i, 256 * i + 256)
        for k1 in range(2):
            value = x_all[s, 2 * k1 + k2].astype(F32)
            total[k1] = total[k1] + jnp.sum(value * value, axis=1, keepdims=True)
            mixed[128 * k1 : 128 * k1 + 128, at] = (value * row).astype(BF16)
        for w in range(2):
            part = dot(mixed[:, at], weights[i][w], 1, 0)
            cols = slice(384 * w, 384 * w + 384)
            acc[:, cols] = part if i == 0 else acc[:, cols] + part
    send[:256] = acc[...].astype(BF16)
    send[256:, :] = jnp.zeros((16, 768), BF16)
    for k1 in range(2):
        head, rest = split_float(jnp.broadcast_to(total[k1], (128, 128)).T[:16])
        send[256:, 128 * k1 : 128 * k1 + 128] = head.astype(BF16)
        send[256:, 256 + 128 * k1 : 384 + 128 * k1] = rest.astype(BF16)


def backward_products_kernel(ids, *refs):
    pieces, weights, (send, mixed, x_all, acc) = refs[:4], refs[4:12], refs[12:]
    for j, s in enumerate((0, 1, 3, 2)):
        x_all[s] = pieces[j][...]
    for i in range(8):
        _, s, k2 = block_place(ids, i)
        at = slice(256 * i, 256 * i + 256)
        for k1 in range(2):
            mixed[128 * k1 : 128 * k1 + 128, at] = x_all[s, 2 * k1 + k2]
        part = dot(mixed[:, at], weights[i][2], 1, 0)
        acc[...] = part if i == 0 else acc[...] + part
    send[...] = acc[...].astype(BF16)


def activations(mine, recv):
    tail = mine[256:257].astype(F32) + recv[256:257].astype(F32)
    total = jnp.concatenate([tail[:, :128] + tail[:, 256:384], tail[:, 128:256] + tail[:, 384:512]])
    cols = [jnp.broadcast_to(total[k : k + 1], (128, 128)).T[:, 0:1] for k in range(2)]
    inv_rms = lax.rsqrt(jnp.concatenate(cols) / 4096 + norm_epsilon)
    pre = (mine[:256].astype(F32) + recv[:256].astype(F32)) * inv_rms
    gate, up = pre[:, :384], pre[:, 384:]
    root = 0.7978845608028654
    tanh = jnp.tanh(root * (gate + 0.044715 * (gate * gate * gate)))
    cdf = 0.5 * (1.0 + tanh)
    slope = cdf + 0.5 * gate * (1.0 - tanh * tanh) * root * (1.0 + 3 * 0.044715 * (gate * gate))
    return inv_rms, gate, up, gate * cdf, slope


def scatter_blocks(ids, held, value):
    for i in range(8):
        _, s, k2 = block_place(ids, i)
        block = value(i).astype(BF16)
        held[s, k2] = block[:128]
        held[s, 2 + k2] = block[128:]


def forward_outputs_kernel(ids, mine, recv, *refs):
    weights, inner, outs, held = refs[:8], refs[8], refs[9:13], refs[13]
    _, _, up, activated, _ = activations(mine, recv)
    inner[...] = (activated * up).astype(BF16)
    scatter_blocks(ids, held, lambda i: dot(inner[...], weights[i][2], 1, 1))
    for s in range(4):
        outs[s][...] = held[s]


def elementwise_kernel(ids, mine, recv, d_mine, d_recv, acts, scale, tail):
    inv_rms, gate, up, activated, slope = activations(mine, recv)
    d_inner = (d_mine[...].astype(F32) + d_recv[...].astype(F32)) * inv_rms
    d_gate = (d_inner * up * slope).astype(BF16)
    d_up = (d_inner * activated).astype(BF16)
    acts[:, :384] = d_gate
    acts[:, 384:] = d_up
    own = (ids[3] // 2) ^ ids[0]
    picked = jnp.where(own == 0, inv_rms[:128], inv_rms[128:])
    scale[...] = jnp.broadcast_to(picked, (128, 128))
    tau = jnp.sum(d_gate.astype(F32) * gate + d_up.astype(F32) * up, axis=1, keepdims=True)
    for k1 in range(2):
        rows = jnp.broadcast_to(tau[128 * k1 : 128 * k1 + 128], (128, 128)).T[:16]
        head, rest = split_float(rows)
        tail[k1, :, :128] = head.astype(BF16)
        tail[k1, :, 128:] = rest.astype(BF16)


def gradients_kernel(ids, acts, inner, tokens, cot, kept, sent):
    for cc, out in ((1, sent), (0, kept)):
        for w in range(3):
            right = inner[...] if w == 2 else acts[:, 384 * w : 384 * w + 384]
            source = cot if w == 2 else tokens
            left = source[:, 1024 * cc : 1024 * cc + 1024]
            out[w] = dot(left, right, 0, 0).astype(BF16).reshape(4, 256, 384)


def backward_outputs_kernel(ids, acts, tail, *refs):
    weights, outs, held = refs[:8], refs[8:12], refs[12]

    def feat(i):
        return dot(acts[:, :384], weights[i][0], 1, 1) + dot(acts[:, 384:], weights[i][1], 1, 1)

    scatter_blocks(ids, held, feat)
    for s in range(4):
        outs[s][:, :128] = held[s]
        for k in range(4):
            outs[s][k, 128:] = tail[k // 2]


def core_sum_kernel(ids, kept, recv, *outs):
    for t in range(4):
        outs[t][...] = (kept[:, t].astype(F32) + recv[:, t].astype(F32)).astype(BF16)


def sum_refs(refs, at):
    total = refs[0][at].astype(F32)
    for ref in refs[1:]:
        total = total + ref[at].astype(F32)
    return total


def x_sum_kernel(first, ids, *refs):
    forward, backward, outs = refs[:4], refs[4:8], refs[8:]
    for k in range(2):
        outs[k][:128] = sum_refs(forward, first + k).astype(BF16)
        outs[k][128:256] = sum_refs(backward, (first + k, slice(0, 128))).astype(BF16)
        tail = sum_refs(backward, (first + k, slice(128, 144)))
        head, rest = split_float(tail[:, :128] + tail[:, 128:])
        outs[k][256:, :128] = head.astype(BF16)
        outs[k][256:, 128:] = rest.astype(BF16)


def scatter_x(parts):
    return [parts[0]] + [shift(parts[s], "x", -s) for s in (2, 1, 3)]


def finish_kernel(ids, p0, p1, p2, p3, tokens, cot, gain, scale, mixed_out, d_tokens):
    parts = (p0, p1, p2, p3)
    local = tokens[...].astype(F32)
    mixed_out[...] = (local + sum_refs(parts, slice(0, 128))).astype(BF16)
    tail = sum_refs(parts, slice(256, 272))
    tau = (tail[:, :128] + tail[:, 128:])[0:1]
    tau = jnp.broadcast_to(tau, (128, 128)).T
    coef = (scale[...] * tau * (1.0 / 4096))[:, 0:1]
    feat = sum_refs(parts, slice(128, 256)) * gain[ids[3] * 4 + ids[4]]
    d_tokens[...] = cot[...].astype(F32) + feat - local * coef


def grads_sum_kernel(ids, p0, p1, p2, p3, grad_gate, grad_up, grad_down):
    parts = (p0, p1, p2, p3)
    grad_gate[...] = sum_refs(parts, 0)
    grad_up[...] = sum_refs(parts, 1)
    grad_down[...] = sum_refs(parts, 2).T


def after(value, *events):
    return lax.optimization_barrier((value, *events))[0]


def on_device(tokens, norm_gain, gate_weight, up_weight, down_weight, out_cotangent):
    ids = jnp.stack([lax.axis_index(n) for n in ("zh", "y", "c", "zl", "x")]).astype(jnp.int32)
    gain = norm_gain.reshape(16, 1, 256)

    pair = jnp.stack([tokens, out_cotangent])
    own = jnp.stack([gate_weight, up_weight, down_weight.T])
    by_z = [lax.ppermute(pair, ("zh", "zl"), z_pairs(k)) for k in range(4)]
    tok_z, cot_z = call(stack_kernel, ids, [by_z[k] for k in (0, 2, 3, 1)], [VMEM] * 4, [((4, 128, 256), BF16)] * 2)
    y1, y3, *_ = lax.optimization_barrier((shift(own, "y", 1), shift(own, "y", 3), *[by_z[k] for k in (0, 2, 3, 1)]))
    y2 = shift(after(own, y1, y3), "y", 2)
    tok_x = [shift(tok_z, "x", s) for s in (1, 3, 2)]
    y2 = after(y2, *tok_x)
    cot_z = after(cot_z, *tok_x)
    tok_x = [tok_z] + tok_x
    by_y = [own, y1, y2, y3]
    weights = by_y + [swap(piece, "c") for piece in by_y]

    x_all = pltpu.VMEM((4, 4, 128, 256), BF16)
    send, tok_all = call(
        forward_products_kernel,
        ids,
        [*tok_x, *weights, gain],
        [VMEM] * 13,
        [((272, 768), BF16), ((256, 2048), BF16)],
        [x_all, pltpu.VMEM((256, 768), F32)],
    )
    cot_x = [cot_z] + [shift(cot_z, "x", s) for s in (1, 3, 2)]
    d_send, cot_all = call(
        backward_products_kernel,
        ids,
        [*cot_x, *weights],
        [VMEM] * 12,
        [((256, 384), BF16), ((256, 2048), BF16)],
        [x_all, pltpu.VMEM((256, 384), F32)],
    )
    recv = swap(send, "zh")
    held = pltpu.VMEM((4, 4, 128, 256), BF16)
    inner, *forward = call(
        forward_outputs_kernel,
        ids,
        [after(send, d_send), recv, *weights],
        [VMEM] * 10,
        [((256, 384), BF16)] + [((4, 128, 256), BF16)] * 4,
        [held],
        8,
        1 << 29,
    )
    forward = scatter_x(forward)
    acts, scale, tail = call(
        elementwise_kernel,
        ids,
        [send, recv, d_send, swap(d_send, "zh")],
        [VMEM] * 4,
        [((256, 768), BF16), ((128, 128), F32), ((2, 16, 256), BF16)],
    )
    backward = call(
        backward_outputs_kernel,
        ids,
        [acts, tail, *weights],
        [VMEM] * 10,
        [((4, 144, 256), BF16)] * 4,
        [held],
        8,
        1 << 30,
    )
    kept, sent = call(
        gradients_kernel,
        ids,
        [acts, after(inner, *forward[1:], backward[0]), tok_all, cot_all],
        [VMEM] * 4,
        [((3, 4, 256, 384), BF16)] * 2,
        (),
        16,
        1 << 31,
    )
    backward = scatter_x(backward)
    sums = list(
        call(core_sum_kernel, ids, [kept, swap(sent, "c")], [VMEM] * 2, [((3, 256, 384), BF16)] * 4)
    )
    near = [shift(sums[1], "y", -1), shift(sums[3], "y", 1)]
    blocks = []
    for k in (0, 2):
        body = functools.partial(x_sum_kernel, k)
        parts = [*forward, *backward]
        blocks += call(body, ids, parts, [VMEM] * 8, [((272, 256), BF16)] * 2)
    blocks[3] = after(blocks[3], *near)
    far = shift(after(sums[2], blocks[2]), "y", 2)
    blocks = [
        lax.ppermute(blocks[k], ("zh", "zl"), [(t, s) for s, t in z_pairs(k)]) for k in range(4)
    ]
    grad_gate, grad_up, grad_down = call(
        grads_sum_kernel,
        ids,
        [sums[0], near[0], far, near[1]],
        [VMEM] * 4,
        [((256, 384), F32), ((256, 384), F32), ((384, 256), F32)],
        (),
        16,
    )
    scale = after(scale, grad_gate)
    mixed_out, d_tokens = call(
        finish_kernel,
        ids,
        [*blocks, tokens, out_cotangent, gain, scale],
        [VMEM] * 8,
        [((128, 256), BF16), ((128, 256), F32)],
    )
    return (mixed_out, d_tokens, grad_gate, grad_up, grad_down)


def solution(mesh):
    split = Mesh(mesh.devices.reshape(2, 4, 2, 4, 4), ("zh", "y", "c", "zl", "x"))
    grp, dev = ("zh", "y", "c"), ("zl", "x")
    in_specs = (P(grp, dev), P(), P(grp, dev), P(grp, dev), P(dev, grp), P(grp, dev))
    out_specs = (P(grp, dev), P(grp, dev), P(grp, dev), P(grp, dev), P(dev, grp))
    return jax.shard_map(
        on_device, mesh=split, in_specs=in_specs, out_specs=out_specs, check_vma=False
    )
```

```python
import functools
import math

import jax
import jax.numpy as jnp
from jax import lax
from jax.experimental import pallas as pl
from jax.experimental.pallas import tpu as pltpu
from jax.sharding import Mesh
from jax.sharding import PartitionSpec as P

norm_epsilon = 1e-06
F32 = jnp.float32
BF16 = jnp.bfloat16
SMEM = pl.BlockSpec(memory_space=pltpu.SMEM)
VMEM = pl.BlockSpec(memory_space=pltpu.VMEM)
MIB = 1 << 20


def dot(left, right, left_dim, right_dim):
    return lax.dot_general(
        left, right, (((left_dim,), (right_dim,)), ((), ())), preferred_element_type=F32
    )


def shift(array, axis, by):
    return lax.ppermute(array, axis, [(i, (i + by) % 4) for i in range(4)])


def swap(array, axis):
    return lax.ppermute(array, axis, [(0, 1), (1, 0)])


def z_pairs(k):
    k1, k2 = k // 2, k % 2
    return [
        (4 * zs + 2 * h + l, 4 * h + 2 * (zs ^ k1) + (l ^ k2))
        for zs in range(2)
        for h in range(2)
        for l in range(2)
    ]


def split_float(value):
    head = value.astype(BF16).astype(F32)
    return head, value - head


def call(body, ids, operands, specs, outs, scratch=(), limit=8, flops=0):
    size = sum(a.size * a.dtype.itemsize for a in operands)
    size += sum(2 * math.prod(shape) for shape, _ in outs)
    return pl.pallas_call(
        body,
        out_shape=[jax.ShapeDtypeStruct(s, d) for s, d in outs],
        in_specs=[SMEM] + specs,
        out_specs=[VMEM] * len(outs),
        scratch_shapes=list(scratch),
        compiler_params=pltpu.CompilerParams(vmem_limit_bytes=limit * MIB),
        cost_estimate=pl.CostEstimate(flops=flops, bytes_accessed=size, transcendentals=0),
    )(ids, *operands)


def block_place(ids, i):
    q = lax.rem(ids[1] - i % 4 + 4, 4) * 2 + (ids[2] ^ (i // 4))
    return q, lax.rem(ids[4] - lax.rem(q, 4) + 4, 4), (ids[3] % 2) ^ (q // 4)


def stack_kernel(ids, p0, p2, p3, p1, tokens, cot):
    for k, piece in enumerate((p0, p1, p2, p3)):
        tokens[k] = piece[0]
        cot[k] = piece[1]


def forward_products_kernel(ids, *refs):
    pieces, weights, (gain, send, mixed, x_all, acc) = refs[:4], refs[4:12], refs[12:]
    for j, s in enumerate((0, 1, 3, 2)):
        x_all[s] = pieces[j][...]
    total = [jnp.zeros((128, 1), F32) for _ in range(2)]
    for i in range(8):
        q, s, k2 = block_place(ids, i)
        row = gain[ids[0] * 8 + q]
        at = slice(256 * i, 256 * i + 256)
        for k1 in range(2):
            value = x_all[s, 2 * k1 + k2].astype(F32)
            total[k1] = total[k1] + jnp.sum(value * value, axis=1, keepdims=True)
            mixed[128 * k1 : 128 * k1 + 128, at] = (value * row).astype(BF16)
        for w in range(2):
            part = dot(mixed[:, at], weights[i][w], 1, 0)
            cols = slice(384 * w, 384 * w + 384)
            acc[:, cols] = part if i == 0 else acc[:, cols] + part
    send[:256] = acc[...].astype(BF16)
    send[256:, :] = jnp.zeros((16, 768), BF16)
    for k1 in range(2):
        head, rest = split_float(jnp.broadcast_to(total[k1], (128, 128)).T[:16])
        send[256:, 128 * k1 : 128 * k1 + 128] = head.astype(BF16)
        send[256:, 256 + 128 * k1 : 384 + 128 * k1] = rest.astype(BF16)


def backward_products_kernel(ids, *refs):
    pieces, weights, (send, mixed, x_all, acc) = refs[:4], refs[4:12], refs[12:]
    for j, s in enumerate((0, 1, 3, 2)):
        x_all[s] = pieces[j][...]
    for i in range(8):
        _, s, k2 = block_place(ids, i)
        at = slice(256 * i, 256 * i + 256)
        for k1 in range(2):
            mixed[128 * k1 : 128 * k1 + 128, at] = x_all[s, 2 * k1 + k2]
        part = dot(mixed[:, at], weights[i][2], 1, 0)
        acc[...] = part if i == 0 else acc[...] + part
    send[...] = acc[...].astype(BF16)


def activations(mine, recv):
    tail = mine[256:257].astype(F32) + recv[256:257].astype(F32)
    total = jnp.concatenate([tail[:, :128] + tail[:, 256:384], tail[:, 128:256] + tail[:, 384:512]])
    cols = [jnp.broadcast_to(total[k : k + 1], (128, 128)).T[:, 0:1] for k in range(2)]
    inv_rms = lax.rsqrt(jnp.concatenate(cols) / 4096 + norm_epsilon)
    pre = (mine[:256].astype(F32) + recv[:256].astype(F32)) * inv_rms
    gate, up = pre[:, :384], pre[:, 384:]
    root = 0.7978845608028654
    tanh = jnp.tanh(root * (gate + 0.044715 * (gate * gate * gate)))
    cdf = 0.5 * (1.0 + tanh)
    slope = cdf + 0.5 * gate * (1.0 - tanh * tanh) * root * (1.0 + 3 * 0.044715 * (gate * gate))
    return inv_rms, gate, up, gate * cdf, slope


def scatter_blocks(ids, held, value):
    for i in range(8):
        _, s, k2 = block_place(ids, i)
        block = value(i).astype(BF16)
        held[s, k2] = block[:128]
        held[s, 2 + k2] = block[128:]


def forward_outputs_kernel(ids, mine, recv, *refs):
    weights, inner, outs, held = refs[:8], refs[8], refs[9:13], refs[13]
    _, _, up, activated, _ = activations(mine, recv)
    inner[...] = (activated * up).astype(BF16)
    scatter_blocks(ids, held, lambda i: dot(inner[...], weights[i][2], 1, 1))
    for s in range(4):
        outs[s][...] = held[s]


def elementwise_kernel(ids, mine, recv, d_mine, d_recv, acts, scale, tail):
    inv_rms, gate, up, activated, slope = activations(mine, recv)
    d_inner = (d_mine[...].astype(F32) + d_recv[...].astype(F32)) * inv_rms
    d_gate = (d_inner * up * slope).astype(BF16)
    d_up = (d_inner * activated).astype(BF16)
    acts[:, :384] = d_gate
    acts[:, 384:] = d_up
    own = (ids[3] // 2) ^ ids[0]
    picked = jnp.where(own == 0, inv_rms[:128], inv_rms[128:])
    scale[...] = jnp.broadcast_to(picked, (128, 128))
    tau = jnp.sum(d_gate.astype(F32) * gate + d_up.astype(F32) * up, axis=1, keepdims=True)
    for k1 in range(2):
        rows = jnp.broadcast_to(tau[128 * k1 : 128 * k1 + 128], (128, 128)).T[:16]
        head, rest = split_float(rows)
        tail[k1, :, :128] = head.astype(BF16)
        tail[k1, :, 128:] = rest.astype(BF16)


def gradients_kernel(ids, acts, inner, tokens, cot, kept, sent):
    for cc, out in ((1, sent), (0, kept)):
        for w in range(3):
            right = inner[...] if w == 2 else acts[:, 384 * w : 384 * w + 384]
            source = cot if w == 2 else tokens
            left = source[:, 1024 * cc : 1024 * cc + 1024]
            out[w] = dot(left, right, 0, 0).astype(BF16).reshape(4, 256, 384)


def backward_outputs_kernel(ids, acts, tail, *refs):
    weights, outs, held = refs[:8], refs[8:12], refs[12]

    def feat(i):
        return dot(acts[:, :384], weights[i][0], 1, 1) + dot(acts[:, 384:], weights[i][1], 1, 1)

    scatter_blocks(ids, held, feat)
    for s in range(4):
        outs[s][:, :128] = held[s]
        for k in range(4):
            outs[s][k, 128:] = tail[k // 2]


def core_sum_kernel(ids, kept, recv, *outs):
    for t in range(4):
        outs[t][...] = (kept[:, t].astype(F32) + recv[:, t].astype(F32)).astype(BF16)


def sum_refs(refs, at):
    total = refs[0][at].astype(F32)
    for ref in refs[1:]:
        total = total + ref[at].astype(F32)
    return total


def x_sum_kernel(chosen, ids, *refs):
    forward, backward, outs = refs[:4], refs[4:8], refs[8:]
    for j, k in enumerate(chosen):
        outs[j][:128] = sum_refs(forward, k).astype(BF16)
        outs[j][128:256] = sum_refs(backward, (k, slice(0, 128))).astype(BF16)
        tail = sum_refs(backward, (k, slice(128, 144)))
        head, rest = split_float(tail[:, :128] + tail[:, 128:])
        outs[j][256:, :128] = head.astype(BF16)
        outs[j][256:, 128:] = rest.astype(BF16)


def scatter_x(parts):
    return [parts[0]] + [shift(parts[s], "x", -s) for s in (2, 1, 3)]


def finish_kernel(ids, p0, p1, p2, p3, tokens, cot, gain, scale, mixed_out, d_tokens):
    parts = (p0, p1, p2, p3)
    local = tokens[...].astype(F32)
    mixed_out[...] = (local + sum_refs(parts, slice(0, 128))).astype(BF16)
    tail = sum_refs(parts, slice(256, 272))
    tau = (tail[:, :128] + tail[:, 128:])[0:1]
    tau = jnp.broadcast_to(tau, (128, 128)).T
    coef = (scale[...] * tau * (1.0 / 4096))[:, 0:1]
    feat = sum_refs(parts, slice(128, 256)) * gain[ids[3] * 4 + ids[4]]
    d_tokens[...] = cot[...].astype(F32) + feat - local * coef


def grads_sum_kernel(ids, p0, p1, p2, p3, grad_gate, grad_up, grad_down):
    parts = (p0, p1, p2, p3)
    grad_gate[...] = sum_refs(parts, 0)
    grad_up[...] = sum_refs(parts, 1)
    grad_down[...] = sum_refs(parts, 2).T


def after(value, *events):
    return lax.optimization_barrier((value, *events))[0]


def on_device(tokens, norm_gain, gate_weight, up_weight, down_weight, out_cotangent):
    ids = jnp.stack([lax.axis_index(n) for n in ("zh", "y", "c", "zl", "x")]).astype(jnp.int32)
    gain = norm_gain.reshape(16, 1, 256)

    pair = jnp.stack([tokens, out_cotangent])
    own = jnp.stack([gate_weight, up_weight, down_weight.T])
    by_z = [lax.ppermute(pair, ("zh", "zl"), z_pairs(k)) for k in range(4)]
    tok_z, cot_z = call(stack_kernel, ids, [by_z[k] for k in (0, 2, 3, 1)], [VMEM] * 4, [((4, 128, 256), BF16)] * 2)
    y1, y3, *_ = lax.optimization_barrier((shift(own, "y", 1), shift(own, "y", 3), *[by_z[k] for k in (0, 2, 3, 1)]))
    y2 = shift(after(own, y1, y3), "y", 2)
    tok_x = [shift(tok_z, "x", s) for s in (1, 3, 2)]
    y2 = after(y2, *tok_x)
    cot_z = after(cot_z, *tok_x)
    tok_x = [tok_z] + tok_x
    by_y = [own, y1, y2, y3]
    weights = by_y + [swap(piece, "c") for piece in by_y]

    x_all = pltpu.VMEM((4, 4, 128, 256), BF16)
    send, tok_all = call(
        forward_products_kernel,
        ids,
        [*tok_x, *weights, gain],
        [VMEM] * 13,
        [((272, 768), BF16), ((256, 2048), BF16)],
        [x_all, pltpu.VMEM((256, 768), F32)],
    )
    cot_x = [cot_z] + [shift(cot_z, "x", s) for s in (1, 3, 2)]
    d_send, cot_all = call(
        backward_products_kernel,
        ids,
        [*cot_x, *weights],
        [VMEM] * 12,
        [((256, 384), BF16), ((256, 2048), BF16)],
        [x_all, pltpu.VMEM((256, 384), F32)],
    )
    recv = swap(send, "zh")
    held = pltpu.VMEM((4, 4, 128, 256), BF16)
    inner, *forward = call(
        forward_outputs_kernel,
        ids,
        [after(send, d_send), recv, *weights],
        [VMEM] * 10,
        [((256, 384), BF16)] + [((4, 128, 256), BF16)] * 4,
        [held],
        8,
        1 << 29,
    )
    forward = scatter_x(forward)
    acts, scale, tail = call(
        elementwise_kernel,
        ids,
        [send, recv, d_send, swap(d_send, "zh")],
        [VMEM] * 4,
        [((256, 768), BF16), ((128, 128), F32), ((2, 16, 256), BF16)],
    )
    backward = call(
        backward_outputs_kernel,
        ids,
        [acts, tail, *weights],
        [VMEM] * 10,
        [((4, 144, 256), BF16)] * 4,
        [held],
        8,
        1 << 30,
    )
    kept, sent = call(
        gradients_kernel,
        ids,
        [acts, after(inner, *forward[1:], backward[0]), tok_all, cot_all],
        [VMEM] * 4,
        [((3, 4, 256, 384), BF16)] * 2,
        (),
        16,
        1 << 31,
    )
    backward = scatter_x(backward)
    sums = list(
        call(core_sum_kernel, ids, [kept, swap(sent, "c")], [VMEM] * 2, [((3, 256, 384), BF16)] * 4)
    )
    near = [shift(sums[1], "y", -1), shift(sums[3], "y", 1)]
    blocks = []
    for chosen in ((1, 3), (2, 0)):
        body = functools.partial(x_sum_kernel, chosen)
        parts = [*forward, *backward]
        blocks += call(body, ids, parts, [VMEM] * 8, [((272, 256), BF16)] * 2)
    blocks[3] = after(blocks[3], *near)
    far = shift(after(sums[2], blocks[2]), "y", 2)
    blocks = [
        lax.ppermute(block, ("zh", "zl"), [(t, s) for s, t in z_pairs(k)])
        for block, k in zip(blocks, (1, 3, 2, 0))
    ]
    grad_gate, grad_up, grad_down = call(
        grads_sum_kernel,
        ids,
        [sums[0], near[0], far, near[1]],
        [VMEM] * 4,
        [((256, 384), F32), ((256, 384), F32), ((384, 256), F32)],
        (),
        16,
    )
    scale = after(scale, grad_gate)
    mixed_out, d_tokens = call(
        finish_kernel,
        ids,
        [*blocks, tokens, out_cotangent, gain, scale],
        [VMEM] * 8,
        [((128, 256), BF16), ((128, 256), F32)],
    )
    return (mixed_out, d_tokens, grad_gate, grad_up, grad_down)


def solution(mesh):
    split = Mesh(mesh.devices.reshape(2, 4, 2, 4, 4), ("zh", "y", "c", "zl", "x"))
    grp, dev = ("zh", "y", "c"), ("zl", "x")
    in_specs = (P(grp, dev), P(), P(grp, dev), P(grp, dev), P(dev, grp), P(grp, dev))
    out_specs = (P(grp, dev), P(grp, dev), P(grp, dev), P(grp, dev), P(dev, grp))
    return jax.shard_map(
        on_device, mesh=split, in_specs=in_specs, out_specs=out_specs, check_vma=False
    )
```
